32 devices in a mesh: grp: 2 (over y), gz: 8 (over z, x), gy: 2 (over core).
Axes of the slice: x: 2, y: 2, z: 4, core: 2. Of those that a mesh axis runs over, the one named last changes fastest.
Arguments:
- estimate_start: float32 [256, 64, 256], P(('grp', 'gz'), 'gy'), parts along dimension 0, may hold values from 0.5 to 2
- view_images: float32 [4, 256, 64, 256], P(None, ('grp', 'gz'), 'gy'), parts along dimension 1, may hold values from 0.5 to 2
- psf_taps: float32 [4, 3, 31], replicated, may hold values from 0.1 to 1
Outputs:
- estimate: float32 [256, 64, 256], P(('grp', 'gz'), 'gy'), parts along dimension 0
The draws below stay inside these ranges and needn't reach their ends.
There are 2 independent parts, one for each index of `grp`. The reference program is written for one: setup_inputs(seed, part) draws one part's arguments, and reference() takes and returns one part's arrays. A program takes and returns all parts, laid end to end along the dimension named above; an argument that names none is the same for every part. Nothing has to cross between parts.
All inputs are finite; a program needn't handle non-finite values.
Results may differ from the reference program's by a relative error of at most 0.00022.
Values sent between devices are 32-bit elements; how exact they have to be, the bound alone decides.
No kernel may reach another device: no remote copies, remote signals or barrier semaphores. Data moves between devices by JAX's collectives and lax.ppermute only.
A program may use at most 64 MiB of HBM per device.

```python
import math
import jax
import jax.numpy as jnp
from jax import lax

X = 256
TAPS = 31
VIEWS = 4
ITERS = 2
Z = 128
Y = 64


def block_scale(own_key, extent, cuts, low, top_value):
    gain = 1.0
    for position, parts in cuts:
        heights = jax.random.uniform(jax.random.fold_in(jax.random.fold_in(own_key, 6), position), (parts,), jnp.float32, low / len(cuts), top_value / len(cuts))
        gain = gain * jnp.repeat(jnp.exp(heights), extent[position] // parts).reshape((-1,) + (1,) * (len(extent) - 1 - position))
    return gain


def setup_inputs(seed: int = 0, part: int = 0) -> dict:
    streams_of = jax.random.split(jax.random.key(seed), 4)
    part_splits = jax.random.split(jax.random.fold_in(streams_of[3], part), 4)
    return {
        "estimate_start": jnp.clip(jnp.exp(math.log(2.0) - 1.3862944 * jax.random.uniform(part_splits[0], (Z, Y, X), jnp.float32) ** block_scale(part_splits[0], (Z, Y, X), ((0, 8), (1, 2)), -0.2, 0.2)), 0.5, 2.0),
        "view_images": jnp.clip(jnp.exp(math.log(2.0) - 1.3862944 * jax.random.uniform(part_splits[1], (VIEWS, Z, Y, X), jnp.float32) ** block_scale(part_splits[1], (VIEWS, Z, Y, X), ((1, 8), (2, 2)), -0.2, 0.2)), 0.5, 2.0),
        "psf_taps": jnp.clip(jnp.exp(jax.random.uniform(streams_of[2], (VIEWS, 3, TAPS), jnp.float32, math.log(0.1), math.log(1.0))), 0.1, 1.0),
    }


def shift_blur(field, kern, axis, sign):
    taps = kern.shape[0]
    half = taps // 2
    length = field.shape[axis]
    widths = [(0, 0)] * field.ndim
    widths[axis] = (half, half)
    padded = jnp.pad(field, widths)
    total = jnp.zeros_like(field)
    for tap in range(taps):
        start = half + sign * (tap - half)
        total = total + kern[tap] * lax.slice_in_dim(padded, start, start + length, axis=axis)
    return total


def reference(estimate_start, view_images, psf_taps):
    estimate = estimate_start
    for view in range(VIEWS):
        kernels = psf_taps[view] / jnp.sum(psf_taps[view], axis=1, keepdims=True)
        for step in range(ITERS):
            blurred = shift_blur(shift_blur(shift_blur(estimate, kernels[2], 2, 1), kernels[1], 1, 1), kernels[0], 0, 1)
            ratio = view_images[view] / blurred
            back = shift_blur(shift_blur(shift_blur(ratio, kernels[2], 2, -1), kernels[1], 1, -1), kernels[0], 0, -1)
            estimate = estimate * back
    return estimate
```

```python
import functools

import jax
import jax.numpy as jnp
from jax import lax
from jax.experimental import pallas as pl
from jax.experimental.pallas import tpu as pltpu
from jax.sharding import PartitionSpec as P

ITERS = 2
AXES = ("gz", "gy")
EDGE = 32
F32, BF16 = jnp.float32, jnp.bfloat16


def spot(zp, xp, c):
    return (2 * zp + xp) * 2 + c


def core_swap(n):
    return [(spot(z, x, c), spot(z, x, 1 - c)) for z in range(n) for x in range(2) for c in range(2)]


def half_swap(n):
    return [(spot(z, x, c), spot(z, 1 - x, c)) for z in range(n) for x in range(2) for c in range(2)]


def chip_swap(n):
    pairs = []
    for x in range(2):
        for z in range(n - 1):
            pairs += [(spot(z, x, 1), spot(z + 1, x, 0)), (spot(z + 1, x, 0), spot(z, x, 1))]
        pairs += [(spot(0, x, 0), spot(0, 1 - x, 0)), (spot(n - 1, x, 1), spot(n - 1, 1 - x, 1))]
    return pairs


def entry_one(n):
    pairs = []
    for z in range(n):
        pairs += [
            (spot(z, 0, 1), spot(z, 0, 0)),
            (spot(z, 0, 0), spot(z, 1, 0)),
            (spot(z, 1, 0), spot(z, 1, 1)),
            (spot(z, 1, 1), spot(z, 0, 1)),
        ]
    return pairs


def entry_two(n):
    pairs = []
    for z in range(n):
        pairs += [
            (spot(z, 0, 0), spot(z, 0, 0)),
            (spot(z, 0, 1), spot(z, 1, 0)),
            (spot(z, 1, 0), spot(z, 0, 1)),
            (spot(z, 1, 1), spot(z, 1, 1)),
        ]
    return pairs


def back(pairs):
    return [(target, source) for source, target in pairs]


def toeplitz(row, size):
    taps, row = row
    base = jnp.concatenate([row, jnp.zeros((1, size - row.shape[1]), F32)], axis=1) if size > row.shape[1] else row
    base = pltpu.roll(jnp.broadcast_to(base, (size, size)), size - taps // 2, 1)
    return pltpu.roll(base, 0, 1, stride=1, stride_axis=0)


def taps_row(taps_ref, index, taps):
    row = taps_ref[index : index + 1]
    return taps, row / jnp.sum(row, axis=1, keepdims=True)


def put_halves(ref, matrix):
    ref[0], ref[1] = split(matrix)


def lanes(shape, axis):
    return lax.broadcasted_iota(jnp.int32, shape, axis)


def mats_kernel(flags, taps_ref, xa_ref, x_ref, y_ref, ya_ref, z_ref, *, index, rows):
    size, wide = xa_ref.shape[1], x_ref.shape[2]
    taps = z_ref.shape[0]
    half = taps // 2
    first = flags[1] == 0

    def within(axis, width):
        lane = lanes((size, size), axis)
        low, high = jnp.where(first, wide + width, wide), jnp.where(first, size, size - width)
        return (lane < low) | (lane >= high)

    band_x = toeplitz(taps_row(taps_ref, index + 2, taps), size)
    held = jnp.where(within(0, EDGE) & within(1, half), band_x, 0.0)
    put_halves(xa_ref, held)
    kept = jnp.where(within(1, half), band_x, 0.0).T
    put_halves(x_ref, kept[:, :wide])
    band_y = toeplitz(taps_row(taps_ref, index + 1, taps), size)
    band_y = jnp.where(lanes((size, size), 0) // rows == lanes((size, size), 1) // rows, band_y, 0.0)
    put_halves(y_ref, band_y)
    put_halves(ya_ref, band_y.T)
    _, row = taps_row(taps_ref, index, taps)
    for tap in range(taps):
        z_ref[tap] = jnp.broadcast_to(row[:, tap : tap + 1], z_ref.shape[1:])


def split(value):
    high = value.astype(BF16)
    return high, (value - high.astype(F32)).astype(BF16)


def dot(a, b):
    return jnp.dot(a, b, preferred_element_type=F32)


def times_right(value, mat_ref):
    high, low = split(value)
    return dot(high, mat_ref[0]) + (dot(low, mat_ref[0]) + dot(high, mat_ref[1]))


def times_left(mat_ref, value):
    high, low = split(value)
    return dot(mat_ref[0], high) + (dot(mat_ref[0], low) + dot(mat_ref[1], high))


def call(kernel, outs, *args, scratch=()):
    def spec(a):
        small = a.ndim == 1
        return pl.BlockSpec(memory_space=pltpu.SMEM if small else pltpu.VMEM)

    return pl.pallas_call(
        kernel,
        out_shape=[jax.ShapeDtypeStruct(s, F32) if isinstance(s, tuple) else s for s in outs],
        in_specs=[spec(a) for a in args],
        out_specs=[pl.BlockSpec(memory_space=pltpu.VMEM) for _ in outs],
        scratch_shapes=list(scratch),
        compiler_params=pltpu.CompilerParams(vmem_limit_bytes=24 * 1024 * 1024),
    )(*args)


def blur_x_kernel(flags, taps_ref, est_ref, one_ref, two_ref, mat_ref, *, taps):
    planes, rows, cols = est_ref.shape
    wide = cols // 2
    band_x = toeplitz(taps_row(taps_ref, 2, taps), cols)
    near = jnp.abs(lanes((cols, cols), 0) - lanes((cols, cols), 1)) <= taps // 2
    put_halves(mat_ref, jnp.where(near, band_x, 0.0).T)
    group = 256 // rows
    lower = flags[0] == 0
    for g in range(planes // group):
        block = est_ref[group * g : group * (g + 1)].reshape(group * rows, cols)
        out = times_right(block, mat_ref)
        low, high = out[:, :wide].reshape(group, rows, wide), out[:, wide:].reshape(group, rows, wide)
        one_ref[group * g : group * (g + 1)] = jnp.where(lower, high, low)
        two_ref[group * g : group * (g + 1)] = jnp.where(lower, low, high)


def join_rows(flags, one_ref, two_ref, out_ref):
    rows = one_ref.shape[1]
    first = flags[1] == 0

    @pl.when(first)
    def _():
        out_ref[:, :rows] = two_ref[...]
        out_ref[:, rows:] = one_ref[...]

    @pl.when(jnp.logical_not(first))
    def _():
        out_ref[:, :rows] = one_ref[...]
        out_ref[:, rows:] = two_ref[...]


def blur_y_kernel(flags, one_ref, two_ref, mat_ref, out_ref):
    join_rows(flags, one_ref, two_ref, out_ref)
    planes, rows, cols = out_ref.shape
    size = mat_ref.shape[1]
    group = size // rows
    for g in range(planes // group):
        block = out_ref[group * g : group * (g + 1)].reshape(size, cols)
        out_ref[group * g : group * (g + 1)] = times_left(mat_ref, block).reshape(group, rows, cols)


def pack_edge(flags, blocks):
    first = jnp.where(flags[1] == 0, EDGE, 0)
    packed = None
    for g, block in enumerate(blocks):
        cols = block.shape[1]
        turned = pltpu.roll(block, (EDGE * g + first) % cols, 1)
        if packed is None:
            packed = turned
        else:
            lane = lax.broadcasted_iota(jnp.int32, block.shape, 1)
            packed = jnp.where(lane // EDGE == g, turned, packed)
    return packed


def open_edge(flags, packed, g):
    cols = packed.shape[1]
    first = jnp.where(flags[1] == 0, 0, cols - EDGE)
    return pltpu.roll(packed, (first + cols - EDGE * g) % cols, 1)


def enter_kernel(flags, one_ref, two_ref, main_ref, edge_ref):
    join_rows(flags, one_ref, two_ref, main_ref)
    planes, rows, cols = main_ref.shape
    groups = cols // EDGE
    each = planes // groups
    edge_ref[...] = pack_edge(
        flags, [main_ref[each * g : each * (g + 1)].reshape(each * rows, cols) for g in range(groups)]
    )


def extend_kernel(flags, main_ref, edge_ref, out_ref):
    planes, rows, cols = main_ref.shape
    groups = cols // EDGE
    each = planes // groups
    for g in range(groups):
        out_ref[each * rows * g : each * rows * (g + 1), :cols] = main_ref[
            each * g : each * (g + 1)
        ].reshape(each * rows, cols)
        out_ref[each * rows * g : each * rows * (g + 1), cols:] = open_edge(flags, edge_ref[...], g)


def update_kernel(flags, back_ref, edge_ref, est_ref, mat_xa, mat_x, mat_y, est_out, part_out):
    planes, rows, cols = back_ref.shape
    groups = cols // EDGE
    each = planes // groups
    size = each * rows
    for g in range(groups):
        at = slice(size * g, size * (g + 1))
        block = back_ref[each * g : each * (g + 1)].reshape(size, cols)
        wide = jnp.concatenate([block, open_edge(flags, edge_ref[...], g)], axis=1)
        est = est_ref[at] * times_right(wide, mat_xa)
        est_out[at] = est
        part = times_left(mat_y, times_right(est, mat_x))
        part_out[each * g : each * (g + 1)] = part.reshape(each, rows, cols)


def last_kernel(flags, back_ref, edge_ref, est_ref, mat_xa, one_out, two_out):
    planes, rows, cols = back_ref.shape
    groups = cols // EDGE
    each = planes // groups
    size = each * rows
    half = rows // 2
    first = flags[1] == 0
    for g in range(groups):
        at = slice(size * g, size * (g + 1))
        block = back_ref[each * g : each * (g + 1)].reshape(size, cols)
        wide = jnp.concatenate([block, open_edge(flags, edge_ref[...], g)], axis=1)
        est = (est_ref[at] * times_right(wide, mat_xa))[:, :cols].reshape(each, rows, cols)
        low, high = est[:, :half], est[:, half:]
        one_out[each * g : each * (g + 1)] = jnp.where(first, high, low)
        two_out[each * g : each * (g + 1)] = jnp.where(first, low, high)


def stack_planes(flags, own_ref, core_ref, chip_ref, stack):
    planes = own_ref.shape[0]
    core = flags[0]
    stack[planes : 2 * planes] = own_ref[...]
    stack[pl.ds((1 - core) * 2 * planes, planes)] = core_ref[...]

    @pl.when(flags[2] == 1)
    def _():
        stack[pl.ds(core * 2 * planes, planes)] = chip_ref[...]

    @pl.when(flags[2] == 0)
    def _():
        stack[pl.ds(core * 2 * planes, planes)] = jnp.zeros(chip_ref.shape, F32)


def along_z(taps_ref, stack, planes, at, flip):
    taps = taps_ref.shape[0]
    half = taps // 2
    field = [stack[planes - half + j, at, :] for j in range(planes + 2 * half)]
    total = [None] * planes
    for tap in range(taps):
        weight = taps_ref[taps - 1 - tap if flip else tap]
        for i in range(planes):
            term = weight * field[i + tap]
            total[i] = term if total[i] is None else total[i] + term
    return total


def ratio_kernel(flags, taps, own_ref, core_ref, chip_ref, one_ref, two_ref, out_ref, stack):
    planes, rows, _ = own_ref.shape
    half = rows // 2
    stack_planes(flags, own_ref, core_ref, chip_ref, stack)
    first = flags[1] == 0

    def step(i, carry):
        for side in range(2):
            at = pl.ds(pl.multiple_of(i * 8 + side * half, 8), 8)
            here = pl.ds(pl.multiple_of(i * 8, 8), 8)
            blurred = along_z(taps, stack, planes, at, False)
            for plane in range(planes):
                one, two = one_ref[plane, here, :], two_ref[plane, here, :]
                view = jnp.where(first, two, one) if side == 0 else jnp.where(first, one, two)
                out_ref[plane, at, :] = view / blurred[plane]
        return carry

    lax.fori_loop(0, half // 8, step, 0)


def back_kernel(flags, taps, own_ref, core_ref, chip_ref, mat_ref, out_ref, edge_ref, stack):
    planes, rows, cols = own_ref.shape
    stack_planes(flags, own_ref, core_ref, chip_ref, stack)

    def step(i, carry):
        at = pl.ds(pl.multiple_of(i * 8, 8), 8)
        total = along_z(taps, stack, planes, at, True)
        for plane in range(planes):
            out_ref[plane, at, :] = total[plane]
        return carry

    lax.fori_loop(0, rows // 8, step, 0)
    groups = cols // EDGE
    each = planes // groups
    blocks = []
    for g in range(groups):
        block = out_ref[each * g : each * (g + 1)].reshape(each * rows, cols)
        block = times_left(mat_ref, block)
        out_ref[each * g : each * (g + 1)] = block.reshape(each, rows, cols)
        blocks.append(block)
    edge_ref[...] = pack_edge(flags, blocks)


def local(estimate_start, view_images, psf_taps):
    planes, rows_dev, cols = estimate_start.shape
    views, _, taps = psf_taps.shape
    n = lax.axis_size("gz") // 2
    rows, wide = rows_dev * lax.axis_size("gy"), cols // 2
    zp, xp, core = lax.axis_index("gz") // 2, lax.axis_index("gz") % 2, lax.axis_index("gy")
    at_end = ((zp == 0) & (core == 0)) | ((zp == n - 1) & (core == 1))
    flags = jnp.stack([core, xp, jnp.where(at_end, 0, 1)]).astype(jnp.int32)
    send = lambda value, pairs: lax.ppermute(value, AXES, pairs)
    field = (planes, rows, wide)
    packed = (planes * rows * EDGE // wide, wide)
    piece = (planes, rows_dev, wide)
    stack = [pltpu.VMEM((3 * planes, rows, wide), F32)]

    rows_y = planes * rows * EDGE // wide
    table = jnp.pad(psf_taps.reshape(views * 3, taps), ((0, 0), (0, wide - taps)))

    def mats(view):
        pair = lambda n, m: jax.ShapeDtypeStruct((2, n, m), BF16)
        return call(
            functools.partial(mats_kernel, index=3 * view, rows=rows),
            [pair(cols, cols), pair(cols, wide), pair(rows_y, rows_y), pair(rows_y, rows_y), (taps, 8, wide)],
            flags, table,
        )

    def pieces(value):
        axis = value.ndim - 1
        return (
            lax.dynamic_slice_in_dim(value, wide * (1 - core), wide, axis),
            lax.dynamic_slice_in_dim(value, wide * core, wide, axis),
        )

    def enter(one, two):
        return send(one, entry_one(n)), send(two, entry_two(n))

    one, two = enter(
        *call(
            functools.partial(blur_x_kernel, taps=taps), [piece, piece], flags, table, estimate_start,
            scratch=[pltpu.VMEM((2, cols, cols), BF16)],
        )
    )
    mat_xa, mat_x, mat_y, mat_ya, k_z = mats(0)
    (part,) = call(blur_y_kernel, [field], flags, one, two, mat_y)
    images = [enter(*pieces(view_images[0]))]
    main, edge = call(enter_kernel, [field, packed], flags, *enter(*pieces(estimate_start)))
    edge = send(edge, half_swap(n))
    (estimate,) = call(extend_kernel, [(planes * rows, 2 * wide)], flags, main, edge)
    for view in range(1, views):
        images.append(enter(*pieces(view_images[view])))

    for view in range(views):
        one, two = images[view]
        for step in range(ITERS):
            ratio, = call(
                ratio_kernel, [field], flags, k_z, part,
                send(part, core_swap(n)), send(part, chip_swap(n)), one, two, scratch=stack,
            )
            corr, edge = call(
                back_kernel, [field, packed], flags, k_z, ratio,
                send(ratio, core_swap(n)), send(ratio, chip_swap(n)), mat_ya, scratch=stack,
            )
            edge = send(edge, half_swap(n))
            if step + 1 < ITERS:
                estimate, part = call(
                    update_kernel, [(planes * rows, 2 * wide), field], flags, corr, edge, estimate, mat_xa, mat_x, mat_y
                )
            elif view + 1 < views:
                old = mat_xa
                mat_xa, mat_x, mat_y, mat_ya, k_z = mats(view + 1)
                estimate, part = call(
                    update_kernel, [(planes * rows, 2 * wide), field], flags, corr, edge, estimate, old, mat_x, mat_y
                )
    one, two = call(last_kernel, [piece, piece], flags, corr, edge, estimate, mat_xa)
    one, two = send(one, back(entry_one(n))), send(two, back(entry_two(n)))
    return jnp.where(
        core == 0, jnp.concatenate([two, one], axis=2), jnp.concatenate([one, two], axis=2)
    )


def solution(mesh):
    return jax.shard_map(
        local,
        mesh=mesh,
        in_specs=(P(("grp", "gz"), "gy", None), P(None, ("grp", "gz"), "gy", None), P()),
        out_specs=P(("grp", "gz"), "gy", None),
        check_vma=False,
    )
```

```python
import functools

import jax
import jax.numpy as jnp
from jax import lax
from jax.experimental import pallas as pl
from jax.experimental.pallas import tpu as pltpu
from jax.sharding import PartitionSpec as P

ITERS = 2
AXES = ("gz", "gy")
EDGE = 32
F32, BF16 = jnp.float32, jnp.bfloat16


def spot(zp, xp, c):
    return (2 * zp + xp) * 2 + c


def core_swap(n):
    return [(spot(z, x, c), spot(z, x, 1 - c)) for z in range(n) for x in range(2) for c in range(2)]


def half_swap(n):
    return [(spot(z, x, c), spot(z, 1 - x, c)) for z in range(n) for x in range(2) for c in range(2)]


def chip_swap(n):
    pairs = []
    for x in range(2):
        for z in range(n - 1):
            pairs += [(spot(z, x, 1), spot(z + 1, x, 0)), (spot(z + 1, x, 0), spot(z, x, 1))]
        pairs += [(spot(0, x, 0), spot(0, 1 - x, 0)), (spot(n - 1, x, 1), spot(n - 1, 1 - x, 1))]
    return pairs


def entry_one(n):
    pairs = []
    for z in range(n):
        pairs += [
            (spot(z, 0, 1), spot(z, 0, 0)),
            (spot(z, 0, 0), spot(z, 1, 0)),
            (spot(z, 1, 0), spot(z, 1, 1)),
            (spot(z, 1, 1), spot(z, 0, 1)),
        ]
    return pairs


def entry_two(n):
    pairs = []
    for z in range(n):
        pairs += [
            (spot(z, 0, 0), spot(z, 0, 0)),
            (spot(z, 0, 1), spot(z, 1, 0)),
            (spot(z, 1, 0), spot(z, 0, 1)),
            (spot(z, 1, 1), spot(z, 1, 1)),
        ]
    return pairs


def back(pairs):
    return [(target, source) for source, target in pairs]


def toeplitz(row, size):
    taps, row = row
    base = jnp.concatenate([row, jnp.zeros((1, size - row.shape[1]), F32)], axis=1) if size > row.shape[1] else row
    base = pltpu.roll(jnp.broadcast_to(base, (size, size)), size - taps // 2, 1)
    return pltpu.roll(base, 0, 1, stride=1, stride_axis=0)


def taps_row(taps_ref, index, taps):
    row = taps_ref[index : index + 1]
    return taps, row / jnp.sum(row, axis=1, keepdims=True)


def put_halves(ref, matrix):
    ref[0], ref[1] = split(matrix)


def lanes(shape, axis):
    return lax.broadcasted_iota(jnp.int32, shape, axis)


def split(value):
    high = value.astype(BF16)
    return high, (value - high.astype(F32)).astype(BF16)


def dot(a, b):
    return jnp.dot(a, b, preferred_element_type=F32)


def times_right(value, mat_ref):
    high, low = split(value)
    return dot(high, mat_ref[0]) + (dot(low, mat_ref[0]) + dot(high, mat_ref[1]))


def times_left(mat_ref, value):
    high, low = split(value)
    return dot(mat_ref[0], high) + (dot(mat_ref[0], low) + dot(mat_ref[1], high))


def call(kernel, outs, *args, scratch=(), cost=0):
    def spec(a):
        small = a.ndim == 1
        return pl.BlockSpec(memory_space=pltpu.SMEM if small else pltpu.VMEM)

    return pl.pallas_call(
        kernel,
        out_shape=[jax.ShapeDtypeStruct(s, F32) if isinstance(s, tuple) else s for s in outs],
        in_specs=[spec(a) for a in args],
        out_specs=[pl.BlockSpec(memory_space=pltpu.VMEM) for _ in outs],
        scratch_shapes=list(scratch),
        compiler_params=pltpu.CompilerParams(vmem_limit_bytes=24 * 1024 * 1024),
        cost_estimate=pl.CostEstimate(flops=1 + cost * 10**9, bytes_accessed=1 + cost * 3 * 10**6, transcendentals=0),
    )(*args)


def blur_x_kernel(flags, taps_ref, est_ref, one_ref, two_ref, mat_ref, *, taps):
    planes, rows, cols = est_ref.shape
    wide = cols // 2
    band_x = toeplitz(taps_row(taps_ref, 2, taps), cols)
    near = jnp.abs(lanes((cols, cols), 0) - lanes((cols, cols), 1)) <= taps // 2
    put_halves(mat_ref, jnp.where(near, band_x, 0.0).T)
    group = 256 // rows
    lower = flags[0] == 0
    for g in range(planes // group):
        block = est_ref[group * g : group * (g + 1)].reshape(group * rows, cols)
        out = times_right(block, mat_ref)
        low, high = out[:, :wide].reshape(group, rows, wide), out[:, wide:].reshape(group, rows, wide)
        one_ref[group * g : group * (g + 1)] = jnp.where(lower, high, low)
        two_ref[group * g : group * (g + 1)] = jnp.where(lower, low, high)


def join_rows(flags, one_ref, two_ref, out_ref):
    rows = one_ref.shape[1]
    first = flags[1] == 0

    @pl.when(first)
    def _():
        out_ref[:, :rows] = two_ref[...]
        out_ref[:, rows:] = one_ref[...]

    @pl.when(jnp.logical_not(first))
    def _():
        out_ref[:, :rows] = one_ref[...]
        out_ref[:, rows:] = two_ref[...]


def put_rows(out_ref, at, block):
    rows = out_ref.shape[2]
    out_ref[0, at], out_ref[1, at] = block[:, :rows], block[:, rows:]


def put_sent(flags, out_ref, core_ref, low_ref, high_ref):
    sent = low_ref.shape[0]
    spare = out_ref.shape[1] - sent
    core_ref[...] = out_ref[:, pl.ds((1 - flags[0]) * spare, sent)]
    at = pl.ds(flags[0] * spare, sent)
    low_ref[...], high_ref[...] = out_ref[0, at], out_ref[1, at]


def blur_y_kernel(flags, one_ref, two_ref, mat_ref, out_ref, core_ref, low_ref, high_ref, joined):
    join_rows(flags, one_ref, two_ref, joined)
    planes, rows, cols = joined.shape
    size = mat_ref.shape[1]
    group = size // rows
    for g in range(planes // group):
        at = slice(group * g, group * (g + 1))
        put_rows(out_ref, at, times_left(mat_ref, joined[at].reshape(size, cols)).reshape(group, rows, cols))
    put_sent(flags, out_ref, core_ref, low_ref, high_ref)


def pack_edge(flags, blocks):
    first = jnp.where(flags[1] == 0, EDGE, 0)
    packed = None
    for g, block in enumerate(blocks):
        cols = block.shape[1]
        turned = pltpu.roll(block, (EDGE * g + first) % cols, 1)
        if packed is None:
            packed = turned
        else:
            lane = lax.broadcasted_iota(jnp.int32, block.shape, 1)
            packed = jnp.where(lane // EDGE == g, turned, packed)
    return packed


def enter_kernel(flags, one_ref, two_ref, main_ref, edge_ref):
    join_rows(flags, one_ref, two_ref, main_ref)
    planes, rows, cols = main_ref.shape
    groups = cols // EDGE
    each = planes // groups
    edge_ref[...] = pack_edge(
        flags, [main_ref[each * g : each * (g + 1)].reshape(each * rows, cols) for g in range(groups)]
    )


def window_kernel(flags, main_ref, edge_ref, out_ref):
    planes, rows, cols = main_ref.shape
    groups = cols // EDGE
    each = planes // groups
    near = EDGE // 2
    own = None
    for g in range(groups):
        block = pltpu.roll(main_ref[each * g : each * (g + 1)].reshape(each * rows, cols), EDGE * g + near, 1)
        own = block if own is None else jnp.where(lanes(block.shape, 1) // EDGE == g, block, own)
    first = flags[1] == 0
    other = pltpu.roll(edge_ref[...], jnp.where(first, near, cols - near), 1)
    left = (lanes(own.shape, 1) % EDGE < near).astype(jnp.int32)
    out_ref[...] = jnp.where(left == jnp.where(first, 1, 0), own, other)


def mats_kernel(
    flags, taps_ref, back_x_ref, back_window_ref, x_ref, window_ref, y_ref, ya_ref, z_ref, full, turned, *, index, rows
):
    size, wide = full.shape[0], x_ref.shape[1]
    taps = z_ref.shape[0]
    groups = wide // EDGE
    near = EDGE // 2
    first = flags[1] == 0
    diff = lanes((size, size), 0) - lanes((size, size), 1)
    band_x = jnp.where(jnp.abs(diff) <= taps // 2, toeplitz(taps_row(taps_ref, index + 2, taps), size), 0.0)
    full[...] = band_x
    turned[...] = band_x.T
    main = pl.ds(pl.multiple_of(flags[1] * wide, wide), wide)
    here = full[main, :]
    block = jnp.where(first, here[:, :wide], here[:, wide:])
    lane = lanes((wide, wide), 1)
    for g in range(groups):
        moved = pltpu.roll(here, (EDGE * g - wide + near) % size, 1)[:, :wide]
        moved = jnp.where(lane // EDGE == g, moved, 0.0)
        put_halves(back_x_ref.at[g], jnp.concatenate([block, moved], axis=1))
    beyond = full[pl.ds(pl.multiple_of(jnp.where(first, wide, wide - EDGE), EDGE), EDGE), :]
    parts = []
    for g in range(groups):
        moved = pltpu.roll(beyond, (EDGE * g - wide + near) % size, 1)[:, :wide]
        parts.append(jnp.where(lanes((EDGE, wide), 1) // EDGE == g, moved, 0.0))
    put_halves(back_window_ref, jnp.concatenate(parts, axis=0))
    here = turned[main, :]
    block = jnp.where(first, here[:, :wide], here[:, wide:])
    row = lanes((wide, wide), 0)
    apart = jnp.where(first, row, row - near)
    put_halves(x_ref, jnp.where((apart >= 0) & (apart < wide - near), block, 0.0))
    around = turned[wide - near : wide + near, :]
    around = jnp.where(first, around[:, :wide], around[:, wide:])
    zero = jnp.zeros((EDGE, wide), F32)
    for pair in range(groups // 2):
        both = [
            jnp.concatenate([around if g == 2 * pair + side else zero for g in range(groups)], axis=0)
            for side in range(2)
        ]
        put_halves(window_ref.at[pair], jnp.concatenate(both, axis=1))
    size = y_ref.shape[1]
    band_y = toeplitz(taps_row(taps_ref, index + 1, taps), size)
    band_y = jnp.where(lanes((size, size), 0) // rows == lanes((size, size), 1) // rows, band_y, 0.0)
    put_halves(y_ref, band_y)
    put_halves(ya_ref, band_y.T)
    _, line = taps_row(taps_ref, index, taps)
    for tap in range(taps):
        z_ref[tap] = jnp.broadcast_to(line[:, tap : tap + 1], z_ref.shape[1:])


def add_planes(total, taps_ref, field, flip):
    taps = taps_ref.shape[0]
    half = taps // 2
    for tap in range(taps):
        weight = None
        for i in range(len(total)):
            plane = field.get(i + tap - half)
            if plane is None:
                continue
            if weight is None:
                weight = taps_ref[taps - 1 - tap if flip else tap]
            term = weight * plane
            total[i] = term if total[i] is None else total[i] + term
    return total


def own_z_kernel(flags, taps, own_ref, core_ref, out_ref, *, flip):
    planes, rows, _ = own_ref.shape
    half = taps.shape[0] // 2
    for core in range(2):

        @pl.when(flags[0] == core)
        def _():
            def step(i, carry):
                at = pl.ds(pl.multiple_of(i * 8, 8), 8)
                field = {j: own_ref[j, at, :] for j in range(planes)}
                for j in range(half):
                    field[planes + j if core == 0 else j - half] = core_ref[j, at, :]
                total = add_planes([None] * planes, taps, field, flip)
                for j in range(planes):
                    out_ref[j, at, :] = total[j]
                return carry

            lax.fori_loop(0, rows // 8, step, 0)


def own_z_both_kernel(flags, taps, own_ref, core_ref, low_ref, high_ref):
    for side, out_ref in enumerate((low_ref, high_ref)):
        own_z_kernel(flags, taps, own_ref.at[side], core_ref.at[side], out_ref, flip=False)


def finish_z(flags, taps, part_ref, chip_ref, flip, put):
    planes, rows, _ = part_ref.shape
    half = chip_ref.shape[0]
    for case in range(3):
        wanted = (flags[2] == 0) if case == 2 else (flags[2] == 1) & (flags[0] == case)

        @pl.when(wanted)
        def _():
            def step(i, carry):
                at = pl.ds(pl.multiple_of(i * 8, 8), 8)
                total = [part_ref[j, at, :] for j in range(planes)]
                if case < 2:
                    first = -half if case == 0 else planes
                    field = {first + j: chip_ref[j, at, :] for j in range(half)}
                    total = add_planes(total, taps, field, flip)
                put(at, total)
                return carry

            lax.fori_loop(0, rows // 8, step, 0)


def ratio_kernel(flags, taps, part_ref, chip_ref, one_ref, two_ref, out_ref, core_ref, send_ref, *, side):
    planes = part_ref.shape[0]
    from_two = flags[1] == side

    def put(at, blurred):
        for j in range(planes):
            out_ref[j, at, :] = jnp.where(from_two, two_ref[j, at, :], one_ref[j, at, :]) / blurred[j]

    finish_z(flags, taps, part_ref, chip_ref, False, put)
    sent = send_ref.shape[0]
    core_ref[...] = out_ref[pl.ds((1 - flags[0]) * (planes - sent), sent)]
    send_ref[...] = out_ref[pl.ds(flags[0] * (planes - sent), sent)]


def back_kernel(flags, taps, part_ref, chip_ref, out_ref):
    def put(at, total):
        for j in range(len(total)):
            out_ref[j, at, :] = total[j]

    finish_z(flags, taps, part_ref, chip_ref, True, put)


def joined_rows(low_ref, high_ref, at):
    block = jnp.concatenate([low_ref[at], high_ref[at]], axis=1)
    return block.reshape(block.shape[0] * block.shape[1], block.shape[2])


def back_edge_kernel(flags, taps, part_ref, chip_ref, low_ref, out_ref, edge_ref):
    back_kernel(flags, taps, part_ref, chip_ref, out_ref)
    planes, rows, cols = out_ref.shape
    groups = cols // EDGE
    each = planes // groups
    edge_ref[...] = pack_edge(
        flags, [joined_rows(low_ref, out_ref, slice(each * g, each * (g + 1))) for g in range(groups)]
    )


def far_kernel(low_ref, high_ref, est_ref, mat_ya, mat_xa, mat_x, mat_y, est_out, corr_out, part_out):
    planes, rows, cols = est_ref.shape
    groups = cols // EDGE
    each = planes // groups
    size = each * rows
    packed = None
    for pair in range(groups // 2):
        both = (2 * pair, 2 * pair + 1)
        block = jnp.concatenate(
            [joined_rows(low_ref, high_ref, slice(each * g, each * (g + 1))) for g in both], axis=1
        )
        block = times_left(mat_ya, block)
        wide = []
        for side, g in enumerate(both):
            corr = times_right(block[:, cols * side : cols * (side + 1)], mat_xa.at[g])
            packed = corr[:, cols:] if packed is None else packed + corr[:, cols:]
            est = est_ref[each * g : each * (g + 1)].reshape(size, cols) * corr[:, :cols]
            est_out[each * g : each * (g + 1)] = est.reshape(each, rows, cols)
            if part_out is not None:
                wide.append(times_right(est, mat_x))
        if part_out is not None:
            part = times_left(mat_y, jnp.concatenate(wide, axis=1))
            for side, g in enumerate(both):
                part_out[each * g : each * (g + 1)] = part[:, cols * side : cols * (side + 1)].reshape(each, rows, cols)
    corr_out[...] = packed


def far_last_kernel(low_ref, high_ref, est_ref, mat_ya, mat_xa, est_out, corr_out):
    far_kernel(low_ref, high_ref, est_ref, mat_ya, mat_xa, None, None, est_out, corr_out, None)


def near_window(edge_ref, corr_ref, window_ref, mat_ya, mat_window):
    edge = times_left(mat_ya, edge_ref[...])
    return window_ref[...] * (corr_ref[...] + times_right(edge, mat_window))


def near_kernel(
    flags, edge_ref, corr_ref, window_ref, part_ref, mat_ya, mat_window, mat_y, mat_around,
    window_out, part_out, core_ref, low_ref, high_ref,
):
    planes, rows, cols = part_ref.shape
    groups = cols // EDGE
    each = planes // groups
    window = near_window(edge_ref, corr_ref, window_ref, mat_ya, mat_window)
    window_out[...] = window
    blurred = times_left(mat_y, window)
    for pair in range(groups // 2):
        share = times_right(blurred, mat_around.at[pair])
        for side in range(2):
            at = slice(each * (2 * pair + side), each * (2 * pair + side + 1))
            put_rows(
                part_out, at, part_ref[at] + share[:, cols * side : cols * (side + 1)].reshape(each, rows, cols)
            )
    put_sent(flags, part_out, core_ref, low_ref, high_ref)


def near_last_kernel(flags, edge_ref, corr_ref, window_ref, est_ref, mat_ya, mat_window, one_out, two_out):
    planes, rows, cols = est_ref.shape
    groups = cols // EDGE
    each = planes // groups
    near = EDGE // 2
    half = rows // 2
    first = flags[1] == 0
    window = near_window(edge_ref, corr_ref, window_ref, mat_ya, mat_window)
    lane = lanes(window.shape, 1)
    apart = jnp.where(first, cols - 1 - lane, lane)
    for g in range(groups):
        at = slice(each * g, each * (g + 1))
        own = pltpu.roll(window, (-EDGE * g - near) % cols, 1)
        est = jnp.where(apart < near, own, est_ref[at].reshape(each * rows, cols)).reshape(each, rows, cols)
        low, high = est[:, :half], est[:, half:]
        one_out[at] = jnp.where(first, high, low)
        two_out[at] = jnp.where(first, low, high)


def local(estimate_start, view_images, psf_taps):
    planes, rows_dev, cols = estimate_start.shape
    views, _, taps = psf_taps.shape
    half = taps // 2
    n = lax.axis_size("gz") // 2
    rows, wide = rows_dev * lax.axis_size("gy"), cols // 2
    zp, xp, core = lax.axis_index("gz") // 2, lax.axis_index("gz") % 2, lax.axis_index("gy")
    at_end = ((zp == 0) & (core == 0)) | ((zp == n - 1) & (core == 1))
    flags = jnp.stack([core, xp, jnp.where(at_end, 0, 1)]).astype(jnp.int32)
    send = lambda value, pairs: lax.ppermute(value, AXES, pairs)
    groups = wide // EDGE
    rows_y = planes * rows // groups
    field, packed, piece = (planes, rows, wide), (rows_y, wide), (planes, rows_dev, wide)
    sent, by_half = (half, rows_dev, wide), (2, *piece)
    sent_both = (2, *sent)
    table = jnp.pad(psf_taps.reshape(views * 3, taps), ((0, 0), (0, wide - taps)))

    def mats(view):
        pair = lambda *shape: jax.ShapeDtypeStruct(shape, BF16)
        return call(
            functools.partial(mats_kernel, index=3 * view, rows=rows),
            [
                pair(groups, 2, wide, 2 * wide),
                pair(2, wide, wide),
                pair(2, wide, wide),
                pair(groups // 2, 2, wide, 2 * wide),
                pair(2, rows_y, rows_y),
                pair(2, rows_y, rows_y),
                (taps, 8, wide),
            ],
            flags, table, scratch=[pltpu.VMEM((cols, cols), F32)] * 2,
        )

    def pieces(value, *index):
        def cut(half):
            start = (*index, 0, 0, wide * half)
            return lax.dynamic_slice(value, start, (1,) * len(index) + piece).reshape(piece)

        return cut(1 - core), cut(core)

    def enter(one, two):
        return send(one, entry_one(n)), send(two, entry_two(n))

    one, two = enter(
        *call(
            functools.partial(blur_x_kernel, taps=taps), [piece, piece], flags, table, estimate_start,
            scratch=[pltpu.VMEM((2, cols, cols), BF16)],
        )
    )
    back_x, back_window, mat_x, around, mat_y, mat_ya, k_z = mats(0)
    part, sent_core, *sent_planes = call(
        blur_y_kernel, [by_half, sent_both, sent, sent], flags, one, two, mat_y, scratch=[pltpu.VMEM(field, F32)]
    )
    image = enter(*pieces(view_images, 0))
    main, edge = call(enter_kernel, [field, packed], flags, *enter(*pieces(estimate_start)))
    edge = send(edge, half_swap(n))
    (window,) = call(window_kernel, [packed], flags, main, edge)

    for view in range(views):
        for step in range(ITERS):
            last = step + 1 == ITERS
            ahead = last and view + 1 < views
            if ahead:
                images, part = lax.optimization_barrier((view_images, part))
                next_one, next_two = pieces(images, view + 1)
                next_one = send(next_one, entry_one(n))
                next_mats = mats(view + 1)
            own = call(own_z_both_kernel, [piece, piece], flags, k_z, part, send(sent_core, core_swap(n)))
            chip = [send(s, chip_swap(n)) for s in sent_planes]
            if ahead:
                chip[1], next_one, next_two = lax.optimization_barrier((chip[1], next_one, next_two))
                next_two = send(next_two, entry_two(n))
            ratio, sent_core, sent_low = call(
                functools.partial(ratio_kernel, side=0), [piece, sent, sent], flags, k_z, own[0], chip[0], *image
            )
            core_low, chip_low = send(sent_core, core_swap(n)), send(sent_low, chip_swap(n))
            chip_high, _ = lax.optimization_barrier((chip[1], ratio))
            (low,) = call(functools.partial(own_z_kernel, flip=True), [piece], flags, k_z, ratio, core_low)
            ratio, sent_core, sent_high = call(
                functools.partial(ratio_kernel, side=1), [piece, sent, sent], flags, k_z, own[1], chip_high, *image
            )
            core_high, chip_high = send(sent_core, core_swap(n)), send(sent_high, chip_swap(n))
            (low,) = call(back_kernel, [piece], flags, k_z, low, chip_low, cost=10)
            core_high, _ = lax.optimization_barrier((core_high, low))
            (high,) = call(functools.partial(own_z_kernel, flip=True), [piece], flags, k_z, ratio, core_high)
            if ahead:
                chip_high, next_two = lax.optimization_barrier((chip_high, next_two))
            high, edge = call(back_edge_kernel, [piece, packed], flags, k_z, high, chip_high, low)
            edge = send(edge, half_swap(n))
            if last and view + 1 == views:
                main, corr = call(far_last_kernel, [field, packed], low, high, main, mat_ya, back_x)
                one, two = call(
                    near_last_kernel, [piece, piece], flags, edge, corr, window, main, mat_ya, back_window
                )
                break
            old_back_x, old_back_window, old_ya = back_x, back_window, mat_ya
            if last:
                back_x, back_window, mat_x, around, mat_y, mat_ya, k_z = next_mats
                image = next_one, next_two
            main, corr, part = call(
                far_kernel, [field, packed, field], low, high, main, old_ya, old_back_x, mat_x, mat_y
            )
            window, part, sent_core, *sent_planes = call(
                near_kernel, [packed, by_half, sent_both, sent, sent],
                flags, edge, corr, window, part, old_ya, old_back_window, mat_y, around,
            )
    one, two = send(one, back(entry_one(n))), send(two, back(entry_two(n)))
    return jnp.where(
        core == 0, jnp.concatenate([two, one], axis=2), jnp.concatenate([one, two], axis=2)
    )


def solution(mesh):
    return jax.shard_map(
        local,
        mesh=mesh,
        in_specs=(P(("grp", "gz"), "gy", None), P(None, ("grp", "gz"), "gy", None), P()),
        out_specs=P(("grp", "gz"), "gy", None),
        check_vma=False,
    )
```

```python
import functools

import jax
import jax.numpy as jnp
from jax import lax
from jax.experimental import pallas as pl
from jax.experimental.pallas import tpu as pltpu
from jax.sharding import PartitionSpec as P

ITERS = 2
AXES = ("gz", "gy")
EDGE = 32
F32, BF16 = jnp.float32, jnp.bfloat16


def spot(zp, xp, c):
    return (2 * zp + xp) * 2 + c


def core_swap(n):
    return [(spot(z, x, c), spot(z, x, 1 - c)) for z in range(n) for x in range(2) for c in range(2)]


def half_swap(n):
    return [(spot(z, x, c), spot(z, 1 - x, c)) for z in range(n) for x in range(2) for c in range(2)]


def chip_swap(n):
    pairs = []
    for x in range(2):
        for z in range(n - 1):
            pairs += [(spot(z, x, 1), spot(z + 1, x, 0)), (spot(z + 1, x, 0), spot(z, x, 1))]
        pairs += [(spot(0, x, 0), spot(0, 1 - x, 0)), (spot(n - 1, x, 1), spot(n - 1, 1 - x, 1))]
    return pairs


def entry_one(n):
    pairs = []
    for z in range(n):
        pairs += [
            (spot(z, 0, 1), spot(z, 0, 0)),
            (spot(z, 0, 0), spot(z, 1, 0)),
            (spot(z, 1, 0), spot(z, 1, 1)),
            (spot(z, 1, 1), spot(z, 0, 1)),
        ]
    return pairs


def entry_two(n):
    pairs = []
    for z in range(n):
        pairs += [
            (spot(z, 0, 0), spot(z, 0, 0)),
            (spot(z, 0, 1), spot(z, 1, 0)),
            (spot(z, 1, 0), spot(z, 0, 1)),
            (spot(z, 1, 1), spot(z, 1, 1)),
        ]
    return pairs


def back(pairs):
    return [(target, source) for source, target in pairs]


def toeplitz(row, half):
    size = row.shape[1]
    base = pltpu.roll(jnp.broadcast_to(row, (size, size)), size - half, 1)
    return pltpu.roll(base, 0, 1, stride=1, stride_axis=0)


def taps_row(taps_ref, view, axis, row_ref):
    taps = taps_ref.shape[2]
    row_ref[...] = jnp.zeros(row_ref.shape, F32)
    row_ref[:, :taps] = taps_ref[view, axis : axis + 1, :]
    row = row_ref[...]
    return row / jnp.sum(row, axis=1, keepdims=True)


def put_halves(ref, matrix):
    ref[0], ref[1] = split(matrix)


def lanes(shape, axis):
    return lax.broadcasted_iota(jnp.int32, shape, axis)


def split(value):
    high = value.astype(BF16)
    return high, (value - high.astype(F32)).astype(BF16)


def dot(a, b):
    return jnp.dot(a, b, preferred_element_type=F32)


def times_right(value, mat_ref):
    high, low = split(value)
    return dot(high, mat_ref[0]) + (dot(low, mat_ref[0]) + dot(high, mat_ref[1]))


def times_left(mat_ref, value):
    high, low = split(value)
    return dot(mat_ref[0], high) + (dot(mat_ref[0], low) + dot(mat_ref[1], high))


def call(kernel, outs, *args, scratch=(), cost=0):
    def spec(a):
        small = a.ndim == 1
        return pl.BlockSpec(memory_space=pltpu.SMEM if small else pltpu.VMEM)

    return pl.pallas_call(
        kernel,
        out_shape=[jax.ShapeDtypeStruct(s, F32) if isinstance(s, tuple) else s for s in outs],
        in_specs=[spec(a) for a in args],
        out_specs=[pl.BlockSpec(memory_space=pltpu.VMEM) for _ in outs],
        scratch_shapes=list(scratch),
        compiler_params=pltpu.CompilerParams(vmem_limit_bytes=24 * 1024 * 1024),
        cost_estimate=pl.CostEstimate(flops=1 + cost * 10**9, bytes_accessed=1 + cost * 3 * 10**6, transcendentals=0),
    )(*args)


def place():
    core, gz, n = lax.axis_index("gy"), lax.axis_index("gz"), lax.axis_size("gz") // 2
    at_end = ((gz < 2) & (core == 0)) | ((gz >= 2 * n - 2) & (core == 1))
    return core, gz % 2, jnp.where(at_end, 0, 1)


def cut_kernel(est_ref, one_ref, two_ref):
    planes, rows, cols = est_ref.shape
    wide = cols // 2
    groups = wide // EDGE
    each = planes // groups
    lower = place()[0] == 0
    packed = None
    for g in range(groups):
        at = slice(each * g, each * (g + 1))
        block = est_ref[at].reshape(each * rows, cols)
        low, high = block[:, :wide].reshape(each, rows, wide), block[:, wide:].reshape(each, rows, wide)
        one_ref[at] = jnp.where(lower, high, low)
        two_ref[at] = jnp.where(lower, low, high)
        turned = pltpu.roll(block, (EDGE * g - wide + EDGE // 2) % cols, 1)[:, :wide]
        packed = turned if packed is None else jnp.where(lanes(turned.shape, 1) // EDGE == g, turned, packed)
    packed = packed.reshape(each, rows, wide)
    one_ref[planes:] = packed
    two_ref[planes:] = packed


def first_kernel(one_ref, two_ref, mat_x, mat_around, mat_y, main_out, window_out, part_out, core_ref, low_ref, high_ref):
    planes, rows, cols = main_out.shape
    half = rows // 2
    first = place()[1] == 0

    @pl.when(first)
    def _():
        main_out[:, :half], main_out[:, half:] = two_ref[:planes], one_ref[:planes]

    @pl.when(jnp.logical_not(first))
    def _():
        main_out[:, :half], main_out[:, half:] = one_ref[:planes], two_ref[:planes]

    one, two = one_ref[planes:], two_ref[planes:]
    groups = cols // EDGE
    each = planes // groups
    size = each * rows
    window = jnp.concatenate([jnp.where(first, two, one), jnp.where(first, one, two)], axis=1).reshape(size, cols)
    window_out[...] = window
    for pair in range(groups // 2):
        both = (2 * pair, 2 * pair + 1)
        blocks = [main_out[each * g : each * (g + 1)].reshape(size, cols) for g in both]
        part = jnp.concatenate([times_right(block, mat_x) for block in blocks], axis=1)
        part = times_left(mat_y, part + times_right(window, mat_around.at[pair]))
        for side, g in enumerate(both):
            put_rows(
                part_out, slice(each * g, each * (g + 1)),
                part[:, cols * side : cols * (side + 1)].reshape(each, rows, cols),
            )
    put_sent(part_out, core_ref, low_ref, high_ref)


def put_rows(out_ref, at, block):
    rows = out_ref.shape[2]
    out_ref[0, at], out_ref[1, at] = block[:, :rows], block[:, rows:]


def put_sent(out_ref, core_ref, low_ref, high_ref):
    flags = place()
    sent = low_ref.shape[0]
    spare = out_ref.shape[1] - sent
    core_ref[...] = out_ref[:, pl.ds((1 - flags[0]) * spare, sent)]
    at = pl.ds(flags[0] * spare, sent)
    low_ref[...], high_ref[...] = out_ref[0, at], out_ref[1, at]


def pack_edge(blocks):
    first = jnp.where(place()[1] == 0, EDGE, 0)
    packed = None
    for g, block in enumerate(blocks):
        cols = block.shape[1]
        turned = pltpu.roll(block, (EDGE * g + first) % cols, 1)
        if packed is None:
            packed = turned
        else:
            lane = lax.broadcasted_iota(jnp.int32, block.shape, 1)
            packed = jnp.where(lane // EDGE == g, turned, packed)
    return packed


def mats_kernel(
    taps_ref, back_x_ref, back_window_ref, x_ref, window_ref, y_ref, ya_ref, z_ref,
    full, turned, row_ref, *, view, rows
):
    size, wide = full.shape[0], x_ref.shape[1]
    taps = z_ref.shape[0]
    groups = wide // EDGE
    near = EDGE // 2
    flags = place()
    first = flags[1] == 0
    diff = lanes((size, size), 0) - lanes((size, size), 1)
    band_x = jnp.where(jnp.abs(diff) <= taps // 2, toeplitz(taps_row(taps_ref, view, 2, row_ref), taps // 2), 0.0)
    full[...] = band_x
    turned[...] = band_x.T
    main = pl.ds(pl.multiple_of(flags[1] * wide, wide), wide)
    here = full[main, :]
    block = jnp.where(first, here[:, :wide], here[:, wide:])
    lane = lanes((wide, wide), 1)
    for g in range(groups):
        moved = pltpu.roll(here, (EDGE * g - wide + near) % size, 1)[:, :wide]
        moved = jnp.where(lane // EDGE == g, moved, 0.0)
        put_halves(back_x_ref.at[g], jnp.concatenate([block, moved], axis=1))
    beyond = full[pl.ds(pl.multiple_of(jnp.where(first, wide, wide - EDGE), EDGE), EDGE), :]
    parts = []
    for g in range(groups):
        moved = pltpu.roll(beyond, (EDGE * g - wide + near) % size, 1)[:, :wide]
        parts.append(jnp.where(lanes((EDGE, wide), 1) // EDGE == g, moved, 0.0))
    put_halves(back_window_ref, jnp.concatenate(parts, axis=0))
    here = turned[main, :]
    block = jnp.where(first, here[:, :wide], here[:, wide:])
    row = lanes((wide, wide), 0)
    apart = jnp.where(first, row, row - near)
    put_halves(x_ref, jnp.where((apart >= 0) & (apart < wide - near), block, 0.0))
    around = turned[wide - near : wide + near, :]
    around = jnp.where(first, around[:, :wide], around[:, wide:])
    zero = jnp.zeros((EDGE, wide), F32)
    for pair in range(groups // 2):
        both = [
            jnp.concatenate([around if g == 2 * pair + side else zero for g in range(groups)], axis=0)
            for side in range(2)
        ]
        put_halves(window_ref.at[pair], jnp.concatenate(both, axis=1))
    band_y = toeplitz(taps_row(taps_ref, view, 1, row_ref), taps // 2)
    band_y = jnp.where(lanes((size, size), 0) // rows == lanes((size, size), 1) // rows, band_y, 0.0)
    put_halves(y_ref, band_y)
    put_halves(ya_ref, band_y.T)
    line = taps_row(taps_ref, view, 0, row_ref)
    for tap in range(taps):
        z_ref[tap] = jnp.broadcast_to(line[:, tap : tap + 1], z_ref.shape[1:])


def add_planes(total, taps_ref, field, flip):
    taps = taps_ref.shape[0]
    half = taps // 2
    for tap in range(taps):
        weight = None
        for i in range(len(total)):
            plane = field.get(i + tap - half)
            if plane is None:
                continue
            if weight is None:
                weight = taps_ref[taps - 1 - tap if flip else tap]
            term = weight * plane
            total[i] = term if total[i] is None else total[i] + term
    return total


def own_z_kernel(taps, own_ref, core_ref, out_ref, *, flip):
    planes, rows, _ = own_ref.shape
    flags = place()
    half = taps.shape[0] // 2
    for core in range(2):

        @pl.when(flags[0] == core)
        def _():
            def step(i, carry):
                at = pl.ds(pl.multiple_of(i * 8, 8), 8)
                field = {j: own_ref[j, at, :] for j in range(planes)}
                for j in range(half):
                    field[planes + j if core == 0 else j - half] = core_ref[j, at, :]
                total = add_planes([None] * planes, taps, field, flip)
                for j in range(planes):
                    out_ref[j, at, :] = total[j]
                return carry

            lax.fori_loop(0, rows // 8, step, 0)


def own_z_both_kernel(taps, own_ref, core_ref, low_ref, high_ref):
    for side, out_ref in enumerate((low_ref, high_ref)):
        own_z_kernel(taps, own_ref.at[side], core_ref.at[side], out_ref, flip=False)


def finish_z(taps, part_ref, chip_ref, flip, put):
    planes, rows, _ = part_ref.shape
    half = chip_ref.shape[0]
    flags = place()
    for case in range(3):
        wanted = (flags[2] == 0) if case == 2 else (flags[2] == 1) & (flags[0] == case)

        @pl.when(wanted)
        def _():
            def step(i, carry):
                at = pl.ds(pl.multiple_of(i * 8, 8), 8)
                total = [part_ref[j, at, :] for j in range(planes)]
                if case < 2:
                    first = -half if case == 0 else planes
                    field = {first + j: chip_ref[j, at, :] for j in range(half)}
                    total = add_planes(total, taps, field, flip)
                put(at, total)
                return carry

            lax.fori_loop(0, rows // 8, step, 0)


def ratio_kernel(taps, part_ref, chip_ref, one_ref, two_ref, out_ref, core_ref, send_ref, *, side):
    planes = part_ref.shape[0]
    flags = place()
    from_two = flags[1] == side

    def put(at, blurred):
        for j in range(planes):
            out_ref[j, at, :] = jnp.where(from_two, two_ref[j, at, :], one_ref[j, at, :]) / blurred[j]

    finish_z(taps, part_ref, chip_ref, False, put)
    sent = send_ref.shape[0]
    core_ref[...] = out_ref[pl.ds((1 - flags[0]) * (planes - sent), sent)]
    send_ref[...] = out_ref[pl.ds(flags[0] * (planes - sent), sent)]


def back_kernel(taps, part_ref, chip_ref, out_ref):
    def put(at, total):
        for j in range(len(total)):
            out_ref[j, at, :] = total[j]

    finish_z(taps, part_ref, chip_ref, True, put)


def joined_rows(low_ref, high_ref, at):
    block = jnp.concatenate([low_ref[at], high_ref[at]], axis=1)
    return block.reshape(block.shape[0] * block.shape[1], block.shape[2])


def back_edge_kernel(taps, part_ref, chip_ref, low_ref, out_ref, edge_ref):
    back_kernel(taps, part_ref, chip_ref, out_ref)
    planes, rows, cols = out_ref.shape
    groups = cols // EDGE
    each = planes // groups
    edge_ref[...] = pack_edge(
        [joined_rows(low_ref, out_ref, slice(each * g, each * (g + 1))) for g in range(groups)]
    )


def far_kernel(low_ref, high_ref, est_ref, mat_ya, mat_xa, mat_x, mat_y, est_out, corr_out, part_out):
    planes, rows, cols = est_ref.shape
    groups = cols // EDGE
    each = planes // groups
    size = each * rows
    packed = None
    for pair in range(groups // 2):
        both = (2 * pair, 2 * pair + 1)
        block = jnp.concatenate(
            [joined_rows(low_ref, high_ref, slice(each * g, each * (g + 1))) for g in both], axis=1
        )
        block = times_left(mat_ya, block)
        wide = []
        for side, g in enumerate(both):
            corr = times_right(block[:, cols * side : cols * (side + 1)], mat_xa.at[g])
            packed = corr[:, cols:] if packed is None else packed + corr[:, cols:]
            est = est_ref[each * g : each * (g + 1)].reshape(size, cols) * corr[:, :cols]
            est_out[each * g : each * (g + 1)] = est.reshape(each, rows, cols)
            if part_out is not None:
                wide.append(times_right(est, mat_x))
        if part_out is not None:
            part = times_left(mat_y, jnp.concatenate(wide, axis=1))
            for side, g in enumerate(both):
                part_out[each * g : each * (g + 1)] = part[:, cols * side : cols * (side + 1)].reshape(each, rows, cols)
    corr_out[...] = packed


def far_last_kernel(low_ref, high_ref, est_ref, mat_ya, mat_xa, est_out, corr_out):
    far_kernel(low_ref, high_ref, est_ref, mat_ya, mat_xa, None, None, est_out, corr_out, None)


def near_window(edge_ref, corr_ref, window_ref, mat_ya, mat_window):
    edge = times_left(mat_ya, edge_ref[...])
    return window_ref[...] * (corr_ref[...] + times_right(edge, mat_window))


def near_kernel(
    edge_ref, corr_ref, window_ref, part_ref, mat_ya, mat_window, mat_y, mat_around,
    window_out, part_out, core_ref, low_ref, high_ref,
):
    planes, rows, cols = part_ref.shape
    groups = cols // EDGE
    each = planes // groups
    window = near_window(edge_ref, corr_ref, window_ref, mat_ya, mat_window)
    window_out[...] = window
    blurred = times_left(mat_y, window)
    for pair in range(groups // 2):
        share = times_right(blurred, mat_around.at[pair])
        for side in range(2):
            at = slice(each * (2 * pair + side), each * (2 * pair + side + 1))
            put_rows(
                part_out, at, part_ref[at] + share[:, cols * side : cols * (side + 1)].reshape(each, rows, cols)
            )
    put_sent(part_out, core_ref, low_ref, high_ref)


def near_last_kernel(edge_ref, corr_ref, window_ref, est_ref, mat_ya, mat_window, one_out, two_out):
    planes, rows, cols = est_ref.shape
    groups = cols // EDGE
    each = planes // groups
    near = EDGE // 2
    half = rows // 2
    first = place()[1] == 0
    window = near_window(edge_ref, corr_ref, window_ref, mat_ya, mat_window)
    lane = lanes(window.shape, 1)
    apart = jnp.where(first, cols - 1 - lane, lane)
    for g in range(groups):
        at = slice(each * g, each * (g + 1))
        own = pltpu.roll(window, (-EDGE * g - near) % cols, 1)
        est = jnp.where(apart < near, own, est_ref[at].reshape(each * rows, cols)).reshape(each, rows, cols)
        low, high = est[:, :half], est[:, half:]
        one_out[at] = jnp.where(first, high, low)
        two_out[at] = jnp.where(first, low, high)


def local(estimate_start, view_images, psf_taps):
    planes, rows_dev, cols = estimate_start.shape
    views, _, taps = psf_taps.shape
    half = taps // 2
    n = lax.axis_size("gz") // 2
    rows, wide = rows_dev * lax.axis_size("gy"), cols // 2
    core = lax.axis_index("gy")
    send = lambda value, pairs: lax.ppermute(value, AXES, pairs)
    groups = wide // EDGE
    rows_y = planes * rows // groups
    field, packed, piece = (planes, rows, wide), (rows_y, wide), (planes, rows_dev, wide)
    sent, by_half = (half, rows_dev, wide), (2, *piece)
    sent_both = (2, *sent)

    def mats(view):
        pair = lambda *shape: jax.ShapeDtypeStruct(shape, BF16)
        return call(
            functools.partial(mats_kernel, view=view, rows=rows),
            [
                pair(groups, 2, wide, 2 * wide),
                pair(2, wide, wide),
                pair(2, wide, wide),
                pair(groups // 2, 2, wide, 2 * wide),
                pair(2, rows_y, rows_y),
                pair(2, rows_y, rows_y),
                (taps, 8, wide),
            ],
            psf_taps, scratch=[pltpu.VMEM((cols, cols), F32)] * 2 + [pltpu.VMEM((1, cols), F32)],
        )

    def pieces(value, *index):
        def cut(half):
            start = (*index, 0, 0, wide * half)
            return lax.dynamic_slice(value, start, (1,) * len(index) + piece).reshape(piece)

        return cut(1 - core), cut(core)

    def enter(one, two):
        return send(one, entry_one(n)), send(two, entry_two(n))

    entry = (planes + planes // groups, rows_dev, wide)
    one, two = enter(*call(cut_kernel, [entry, entry], estimate_start))
    back_x, back_window, mat_x, around, mat_y, mat_ya, k_z = mats(0)
    image = enter(*pieces(view_images, 0))
    main, window, part, sent_core, *sent_planes = call(
        first_kernel, [field, packed, by_half, sent_both, sent, sent], one, two, mat_x, around, mat_y
    )

    for view in range(views):
        for step in range(ITERS):
            last = step + 1 == ITERS
            ahead = last and view + 1 < views
            if ahead:
                images, part = lax.optimization_barrier((view_images, part))
                next_one, next_two = pieces(images, view + 1)
                next_one = send(next_one, entry_one(n))
            own = call(own_z_both_kernel, [piece, piece], k_z, part, send(sent_core, core_swap(n)))
            chip = [send(s, chip_swap(n)) for s in sent_planes]
            if view + 1 < views and not last:
                chip[0], *next_mats = lax.optimization_barrier((chip[0], *mats(view + 1)))
            if ahead:
                chip[1], next_one, next_two = lax.optimization_barrier((chip[1], next_one, next_two))
                next_two = send(next_two, entry_two(n))
            ratio, sent_core, sent_low = call(
                functools.partial(ratio_kernel, side=0), [piece, sent, sent], k_z, own[0], chip[0], *image
            )
            core_low, chip_low = send(sent_core, core_swap(n)), send(sent_low, chip_swap(n))
            chip_high, _ = lax.optimization_barrier((chip[1], ratio))
            (low,) = call(functools.partial(own_z_kernel, flip=True), [piece], k_z, ratio, core_low)
            ratio, sent_core, sent_high = call(
                functools.partial(ratio_kernel, side=1), [piece, sent, sent], k_z, own[1], chip_high, *image
            )
            core_high, chip_high = send(sent_core, core_swap(n)), send(sent_high, chip_swap(n))
            (low,) = call(back_kernel, [piece], k_z, low, chip_low, cost=10)
            core_high, _ = lax.optimization_barrier((core_high, low))
            (high,) = call(functools.partial(own_z_kernel, flip=True), [piece], k_z, ratio, core_high)
            if ahead:
                chip_high, next_two = lax.optimization_barrier((chip_high, next_two))
            high, edge = call(back_edge_kernel, [piece, packed], k_z, high, chip_high, low)
            edge = send(edge, half_swap(n))
            if last and view + 1 == views:
                main, corr = call(far_last_kernel, [field, packed], low, high, main, mat_ya, back_x)
                one, two = call(
                    near_last_kernel, [piece, piece], edge, corr, window, main, mat_ya, back_window
                )
                break
            old_back_x, old_back_window, old_ya = back_x, back_window, mat_ya
            if last:
                back_x, back_window, mat_x, around, mat_y, mat_ya, k_z = next_mats
                image = next_one, next_two
            main, corr, part = call(
                far_kernel, [field, packed, field], low, high, main, old_ya, old_back_x, mat_x, mat_y
            )
            window, part, sent_core, *sent_planes = call(
                near_kernel, [packed, by_half, sent_both, sent, sent],
                edge, corr, window, part, old_ya, old_back_window, mat_y, around,
            )
    one, two = send(one, back(entry_one(n))), send(two, back(entry_two(n)))
    return jnp.where(
        core == 0, jnp.concatenate([two, one], axis=2), jnp.concatenate([one, two], axis=2)
    )


def solution(mesh):
    return jax.shard_map(
        local,
        mesh=mesh,
        in_specs=(P(("grp", "gz"), "gy", None), P(None, ("grp", "gz"), "gy", None), P()),
        out_specs=P(("grp", "gz"), "gy", None),
        check_vma=False,
    )
```

```python
import functools

import jax
import jax.numpy as jnp
from jax import lax
from jax.experimental import pallas as pl
from jax.experimental.pallas import tpu as pltpu
from jax.sharding import PartitionSpec as P

ITERS = 2
AXES = ("gz", "gy")
EDGE = 32
F32, BF16 = jnp.float32, jnp.bfloat16


def spot(zp, xp, c):
    return (2 * zp + xp) * 2 + c


def core_swap(n):
    return [(spot(z, x, c), spot(z, x, 1 - c)) for z in range(n) for x in range(2) for c in range(2)]


def half_swap(n):
    return [(spot(z, x, c), spot(z, 1 - x, c)) for z in range(n) for x in range(2) for c in range(2)]


def chip_swap(n):
    pairs = []
    for x in range(2):
        for z in range(n - 1):
            pairs += [(spot(z, x, 1), spot(z + 1, x, 0)), (spot(z + 1, x, 0), spot(z, x, 1))]
        pairs += [(spot(0, x, 0), spot(0, 1 - x, 0)), (spot(n - 1, x, 1), spot(n - 1, 1 - x, 1))]
    return pairs


def entry_one(n):
    pairs = []
    for z in range(n):
        pairs += [
            (spot(z, 0, 1), spot(z, 0, 0)),
            (spot(z, 0, 0), spot(z, 1, 0)),
            (spot(z, 1, 0), spot(z, 1, 1)),
            (spot(z, 1, 1), spot(z, 0, 1)),
        ]
    return pairs


def entry_two(n, over_z):
    pairs = []
    for z in range(n):
        pairs += [(spot(z, 0, 1), spot(z, 1, 0)), (spot(z, 1, 0), spot(z, 0, 1))]
        if over_z and n % 2 == 0:
            pairs += [(spot(z, 0, 0), spot(z ^ 1, 0, 0)), (spot(z, 1, 1), spot(z ^ 1, 1, 1))]
        else:
            pairs += [(spot(z, 0, 0), spot(z, 1, 1)), (spot(z, 1, 1), spot(z, 0, 0))]
    return pairs


def back(pairs):
    return [(target, source) for source, target in pairs]


def toeplitz(row, half):
    size = row.shape[1]
    base = pltpu.roll(jnp.broadcast_to(row, (size, size)), size - half, 1)
    return pltpu.roll(base, 0, 1, stride=1, stride_axis=0)


def taps_row(taps_ref, view, axis, row_ref):
    taps = taps_ref.shape[2]
    row_ref[...] = jnp.zeros(row_ref.shape, F32)
    row_ref[:, :taps] = taps_ref[view, axis : axis + 1, :]
    row = row_ref[...]
    return row / jnp.sum(row, axis=1, keepdims=True)


def put_halves(ref, matrix):
    ref[0], ref[1] = split(matrix)


def lanes(shape, axis):
    return lax.broadcasted_iota(jnp.int32, shape, axis)


def split(value):
    high = value.astype(BF16)
    return high, (value - high.astype(F32)).astype(BF16)


def dot(a, b):
    return jnp.dot(a, b, preferred_element_type=F32)


def times_right(value, mat_ref):
    high, low = split(value)
    return dot(high, mat_ref[0]) + (dot(low, mat_ref[0]) + dot(high, mat_ref[1]))


def times_left(mat_ref, value):
    high, low = split(value)
    return dot(mat_ref[0], high) + (dot(mat_ref[0], low) + dot(mat_ref[1], high))


def call(kernel, outs, *args, scratch=(), cost=0):
    def spec(a):
        small = a.ndim == 1
        return pl.BlockSpec(memory_space=pltpu.SMEM if small else pltpu.VMEM)

    return pl.pallas_call(
        kernel,
        out_shape=[jax.ShapeDtypeStruct(s, F32) if isinstance(s, tuple) else s for s in outs],
        in_specs=[spec(a) for a in args],
        out_specs=[pl.BlockSpec(memory_space=pltpu.VMEM) for _ in outs],
        scratch_shapes=list(scratch),
        compiler_params=pltpu.CompilerParams(vmem_limit_bytes=24 * 1024 * 1024),
        cost_estimate=pl.CostEstimate(flops=1 + cost * 10**9, bytes_accessed=1 + cost * 3 * 10**6, transcendentals=0),
    )(*args)


def place():
    core, gz, n = lax.axis_index("gy"), lax.axis_index("gz"), lax.axis_size("gz") // 2
    at_end = ((gz < 2) & (core == 0)) | ((gz >= 2 * n - 2) & (core == 1))
    return core, gz % 2, jnp.where(at_end, 0, 1)


def cut_kernel(est_ref, one_ref, two_ref):
    planes, rows, cols = est_ref.shape
    wide = cols // 2
    groups = wide // EDGE
    each = planes // groups
    lower = place()[0] == 0
    packed = None
    for g in range(groups):
        at = slice(each * g, each * (g + 1))
        block = est_ref[at].reshape(each * rows, cols)
        low, high = block[:, :wide].reshape(each, rows, wide), block[:, wide:].reshape(each, rows, wide)
        one_ref[at] = jnp.where(lower, high, low)
        two_ref[at] = jnp.where(lower, low, high)
        turned = pltpu.roll(block, (EDGE * g - wide + EDGE // 2) % cols, 1)[:, :wide]
        packed = turned if packed is None else jnp.where(lanes(turned.shape, 1) // EDGE == g, turned, packed)
    packed = packed.reshape(each, rows, wide)
    one_ref[planes:] = packed
    two_ref[planes:] = packed


def first_kernel(
    one_ref, two_ref, kept_ref, mat_x, mat_around, mat_y,
    main_out, window_out, part_out, core_low_ref, core_high_ref, low_ref, high_ref,
):
    planes, rows, cols = main_out.shape
    half = rows // 2
    first = place()[1] == 0

    one, two = one_ref[...], jnp.where(stays(), kept_ref[...], two_ref[...])
    low, high = jnp.where(first, two, one), jnp.where(first, one, two)
    main_out[:, :half], main_out[:, half:] = low[:planes], high[:planes]
    groups = cols // EDGE
    each = planes // groups
    size = each * rows
    window = jnp.concatenate([low[planes:], high[planes:]], axis=1).reshape(size, cols)
    window_out[...] = window
    for pair in range(groups // 2):
        both = (2 * pair, 2 * pair + 1)
        blocks = [main_out[each * g : each * (g + 1)].reshape(size, cols) for g in both]
        part = jnp.concatenate([times_right(block, mat_x) for block in blocks], axis=1)
        part = times_left(mat_y, part + times_right(window, mat_around.at[pair]))
        for side, g in enumerate(both):
            put_rows(
                part_out, slice(each * g, each * (g + 1)),
                part[:, cols * side : cols * (side + 1)].reshape(each, rows, cols),
            )
    put_sent(part_out, (core_low_ref, core_high_ref), low_ref, high_ref)


def stays():
    core, xp, _ = place()
    return core == xp


def put_rows(out_ref, at, block):
    rows = out_ref.shape[2]
    out_ref[0, at], out_ref[1, at] = block[:, :rows], block[:, rows:]


def put_sent(out_ref, core_ref, low_ref, high_ref):
    flags = place()
    sent = low_ref.shape[0]
    spare = out_ref.shape[1] - sent
    at = pl.ds((1 - flags[0]) * spare, sent)
    core_ref[0][...], core_ref[1][...] = out_ref[0, at], out_ref[1, at]
    at = pl.ds(flags[0] * spare, sent)
    low_ref[...], high_ref[...] = out_ref[0, at], out_ref[1, at]


def pack_edge(blocks):
    first = jnp.where(place()[1] == 0, EDGE, 0)
    packed = None
    for g, block in enumerate(blocks):
        cols = block.shape[1]
        turned = pltpu.roll(block, (EDGE * g + first) % cols, 1)
        if packed is None:
            packed = turned
        else:
            lane = lax.broadcasted_iota(jnp.int32, block.shape, 1)
            packed = jnp.where(lane // EDGE == g, turned, packed)
    return packed


def mats_kernel(
    taps_ref, back_x_ref, back_window_ref, x_ref, window_ref, y_ref, ya_ref, z_ref,
    full, turned, row_ref, *, view, rows
):
    size, wide = full.shape[0], x_ref.shape[1]
    taps = z_ref.shape[0]
    groups = wide // EDGE
    near = EDGE // 2
    flags = place()
    first = flags[1] == 0
    diff = lanes((size, size), 0) - lanes((size, size), 1)
    band_x = jnp.where(jnp.abs(diff) <= taps // 2, toeplitz(taps_row(taps_ref, view, 2, row_ref), taps // 2), 0.0)
    full[...] = band_x
    turned[...] = band_x.T
    main = pl.ds(pl.multiple_of(flags[1] * wide, wide), wide)
    here = full[main, :]
    block = jnp.where(first, here[:, :wide], here[:, wide:])
    lane = lanes((wide, wide), 1)
    for g in range(groups):
        moved = pltpu.roll(here, (EDGE * g - wide + near) % size, 1)[:, :wide]
        moved = jnp.where(lane // EDGE == g, moved, 0.0)
        put_halves(back_x_ref.at[g], jnp.concatenate([block, moved], axis=1))
    beyond = full[pl.ds(pl.multiple_of(jnp.where(first, wide, wide - EDGE), EDGE), EDGE), :]
    parts = []
    for g in range(groups):
        moved = pltpu.roll(beyond, (EDGE * g - wide + near) % size, 1)[:, :wide]
        parts.append(jnp.where(lanes((EDGE, wide), 1) // EDGE == g, moved, 0.0))
    put_halves(back_window_ref, jnp.concatenate(parts, axis=0))
    here = turned[main, :]
    block = jnp.where(first, here[:, :wide], here[:, wide:])
    row = lanes((wide, wide), 0)
    apart = jnp.where(first, row, row - near)
    put_halves(x_ref, jnp.where((apart >= 0) & (apart < wide - near), block, 0.0))
    around = turned[wide - near : wide + near, :]
    around = jnp.where(first, around[:, :wide], around[:, wide:])
    zero = jnp.zeros((EDGE, wide), F32)
    for pair in range(groups // 2):
        both = [
            jnp.concatenate([around if g == 2 * pair + side else zero for g in range(groups)], axis=0)
            for side in range(2)
        ]
        put_halves(window_ref.at[pair], jnp.concatenate(both, axis=1))
    band_y = toeplitz(taps_row(taps_ref, view, 1, row_ref), taps // 2)
    band_y = jnp.where(lanes((size, size), 0) // rows == lanes((size, size), 1) // rows, band_y, 0.0)
    put_halves(y_ref, band_y)
    put_halves(ya_ref, band_y.T)
    line = taps_row(taps_ref, view, 0, row_ref)
    for tap in range(taps):
        z_ref[tap] = jnp.broadcast_to(line[:, tap : tap + 1], z_ref.shape[1:])


def add_planes(total, taps_ref, field, flip):
    taps = taps_ref.shape[0]
    half = taps // 2
    for tap in range(taps):
        weight = None
        for i in range(len(total)):
            plane = field.get(i + tap - half)
            if plane is None:
                continue
            if weight is None:
                weight = taps_ref[taps - 1 - tap if flip else tap]
            term = weight * plane
            total[i] = term if total[i] is None else total[i] + term
    return total


def own_z_kernel(taps, own_ref, core_ref, out_ref, *, flip):
    planes, rows, _ = own_ref.shape
    flags = place()
    half = taps.shape[0] // 2
    for core in range(2):

        @pl.when(flags[0] == core)
        def _():
            def step(i, carry):
                at = pl.ds(pl.multiple_of(i * 8, 8), 8)
                field = {j: own_ref[j, at, :] for j in range(planes)}
                for j in range(half):
                    field[planes + j if core == 0 else j - half] = core_ref[j, at, :]
                total = add_planes([None] * planes, taps, field, flip)
                for j in range(planes):
                    out_ref[j, at, :] = total[j]
                return carry

            lax.fori_loop(0, rows // 8, step, 0)


def own_z_both_kernel(taps, own_ref, core_ref, low_ref, high_ref):
    for side, out_ref in enumerate((low_ref, high_ref)):
        own_z_kernel(taps, own_ref.at[side], core_ref.at[side], out_ref, flip=False)


def own_z_first_kernel(taps, own_ref, core_low_ref, core_high_ref, low_ref, high_ref):
    own_z_kernel(taps, own_ref.at[0], core_low_ref, low_ref, flip=False)
    own_z_kernel(taps, own_ref.at[1], core_high_ref, high_ref, flip=False)


def finish_z(taps, part_ref, chip_ref, flip, put):
    planes, rows, _ = part_ref.shape
    half = chip_ref.shape[0]
    flags = place()
    for case in range(3):
        wanted = (flags[2] == 0) if case == 2 else (flags[2] == 1) & (flags[0] == case)

        @pl.when(wanted)
        def _():
            def step(i, carry):
                at = pl.ds(pl.multiple_of(i * 8, 8), 8)
                total = [part_ref[j, at, :] for j in range(planes)]
                if case < 2:
                    first = -half if case == 0 else planes
                    field = {first + j: chip_ref[j, at, :] for j in range(half)}
                    total = add_planes(total, taps, field, flip)
                put(at, total)
                return carry

            lax.fori_loop(0, rows // 8, step, 0)


def ratio_kernel(taps, part_ref, chip_ref, one_ref, two_ref, kept_ref, out_ref, core_ref, send_ref, *, side):
    planes = part_ref.shape[0]
    flags = place()
    from_two, keep = flags[1] == side, stays()

    def put(at, blurred):
        for j in range(planes):
            two = jnp.where(keep, kept_ref[j, at, :], two_ref[j, at, :])
            out_ref[j, at, :] = jnp.where(from_two, two, one_ref[j, at, :]) / blurred[j]

    finish_z(taps, part_ref, chip_ref, False, put)
    sent = send_ref.shape[0]
    core_ref[...] = out_ref[pl.ds((1 - flags[0]) * (planes - sent), sent)]
    send_ref[...] = out_ref[pl.ds(flags[0] * (planes - sent), sent)]


def back_kernel(taps, part_ref, chip_ref, out_ref):
    def put(at, total):
        for j in range(len(total)):
            out_ref[j, at, :] = total[j]

    finish_z(taps, part_ref, chip_ref, True, put)


def joined_rows(low_ref, high_ref, at):
    block = jnp.concatenate([low_ref[at], high_ref[at]], axis=1)
    return block.reshape(block.shape[0] * block.shape[1], block.shape[2])


def back_edge_kernel(taps, part_ref, chip_ref, out_ref, edge_ref):
    back_kernel(taps, part_ref, chip_ref, out_ref)
    planes, rows, cols = out_ref.shape
    groups = cols // EDGE
    each = planes // groups
    packed = pack_edge([out_ref[each * g : each * (g + 1)].reshape(each * rows, cols) for g in range(groups)])
    edge_ref[...] = packed.reshape(edge_ref.shape)


def far_kernel(low_ref, high_ref, est_ref, mat_ya, mat_xa, mat_x, mat_y, est_out, corr_out, part_out):
    planes, rows, cols = est_ref.shape
    groups = cols // EDGE
    each = planes // groups
    size = each * rows
    packed = None
    for pair in range(groups // 2):
        both = (2 * pair, 2 * pair + 1)
        block = jnp.concatenate(
            [joined_rows(low_ref, high_ref, slice(each * g, each * (g + 1))) for g in both], axis=1
        )
        block = times_left(mat_ya, block)
        wide = []
        for side, g in enumerate(both):
            corr = times_right(block[:, cols * side : cols * (side + 1)], mat_xa.at[g])
            packed = corr[:, cols:] if packed is None else packed + corr[:, cols:]
            est = est_ref[each * g : each * (g + 1)].reshape(size, cols) * corr[:, :cols]
            est_out[each * g : each * (g + 1)] = est.reshape(each, rows, cols)
            if part_out is not None:
                wide.append(times_right(est, mat_x))
        if part_out is not None:
            part = times_left(mat_y, jnp.concatenate(wide, axis=1))
            for side, g in enumerate(both):
                part_out[each * g : each * (g + 1)] = part[:, cols * side : cols * (side + 1)].reshape(each, rows, cols)
    corr_out[...] = packed


def far_last_kernel(low_ref, high_ref, est_ref, mat_ya, mat_xa, one_out, two_out, corr_out, est):
    far_kernel(low_ref, high_ref, est_ref, mat_ya, mat_xa, None, None, est, corr_out, None)
    half = est.shape[1] // 2
    first = place()[1] == 0
    low, high = est[:, :half], est[:, half:]
    one_out[...] = jnp.where(first, high, low)
    two_out[...] = jnp.where(first, low, high)


def near_window(edge_low, edge_high, corr_ref, window_ref, mat_ya, mat_window):
    edge = times_left(mat_ya, joined_rows(edge_low, edge_high, slice(None)))
    return window_ref[...] * (corr_ref[...] + times_right(edge, mat_window))


def near_kernel(
    edge_low, edge_high, corr_ref, window_ref, part_ref, mat_ya, mat_window, mat_y, mat_around,
    window_out, part_out, core_ref, low_ref, high_ref,
):
    planes, rows, cols = part_ref.shape
    groups = cols // EDGE
    each = planes // groups
    window = near_window(edge_low, edge_high, corr_ref, window_ref, mat_ya, mat_window)
    window_out[...] = window
    blurred = times_left(mat_y, window)
    for pair in range(groups // 2):
        share = times_right(blurred, mat_around.at[pair])
        for side in range(2):
            at = slice(each * (2 * pair + side), each * (2 * pair + side + 1))
            put_rows(
                part_out, at, part_ref[at] + share[:, cols * side : cols * (side + 1)].reshape(each, rows, cols)
            )
    put_sent(part_out, (core_ref.at[0], core_ref.at[1]), low_ref, high_ref)


def near_last_kernel(edge_low, edge_high, corr_ref, window_ref, mat_ya, mat_window, out_ref):
    window = near_window(edge_low, edge_high, corr_ref, window_ref, mat_ya, mat_window)
    each, half, cols = out_ref.shape
    window = window.reshape(each, 2 * half, cols)
    out_ref[...] = jnp.where(place()[1] == 0, window[:, :half], window[:, half:])


def leave_kernel(one_ref, two_ref, kept_ref, window_ref, window_kept_ref, out_ref):
    planes, rows, wide = one_ref.shape
    groups = wide // EDGE
    each = planes // groups
    lower = place()[0] == 0
    one, two = one_ref[...], jnp.where(stays(), kept_ref[...], two_ref[...])
    window = jnp.where(stays(), window_kept_ref[...], window_ref[...]).reshape(each * rows, wide)
    window = jnp.concatenate([window, window], axis=1)
    from_cut = lanes(window.shape, 1) - wide + EDGE // 2
    for g in range(groups):
        at = slice(each * g, each * (g + 1))
        block = jnp.concatenate([jnp.where(lower, two[at], one[at]), jnp.where(lower, one[at], two[at])], axis=2)
        turned = pltpu.roll(window, (wide - EDGE // 2 - EDGE * g) % (2 * wide), 1)
        block = jnp.where((from_cut >= 0) & (from_cut < EDGE), turned, block.reshape(each * rows, 2 * wide))
        out_ref[at] = block.reshape(each, rows, 2 * wide)


def local(estimate_start, view_images, psf_taps):
    planes, rows_dev, cols = estimate_start.shape
    views, _, taps = psf_taps.shape
    half = taps // 2
    n = lax.axis_size("gz") // 2
    rows, wide = rows_dev * lax.axis_size("gy"), cols // 2
    core = lax.axis_index("gy")
    send = lambda value, pairs: lax.ppermute(value, AXES, pairs)
    groups = wide // EDGE
    rows_y = planes * rows // groups
    field, packed, piece = (planes, rows, wide), (rows_y, wide), (planes, rows_dev, wide)
    sent, by_half = (half, rows_dev, wide), (2, *piece)
    sent_both, edge = (2, *sent), (planes // groups, rows_dev, wide)

    def mats(view):
        pair = lambda *shape: jax.ShapeDtypeStruct(shape, BF16)
        return call(
            functools.partial(mats_kernel, view=view, rows=rows),
            [
                pair(groups, 2, wide, 2 * wide),
                pair(2, wide, wide),
                pair(2, wide, wide),
                pair(groups // 2, 2, wide, 2 * wide),
                pair(2, rows_y, rows_y),
                pair(2, rows_y, rows_y),
                (taps, 8, wide),
            ],
            psf_taps, scratch=[pltpu.VMEM((cols, cols), F32)] * 2 + [pltpu.VMEM((1, cols), F32)],
        )

    def pieces(value, *index):
        def cut(half):
            start = (*index, 0, 0, wide * half)
            return lax.dynamic_slice(value, start, (1,) * len(index) + piece).reshape(piece)

        return cut(1 - core), cut(core)

    entry = (planes + planes // groups, rows_dev, wide)
    one, kept = call(cut_kernel, [entry, entry], estimate_start)
    one, two = send(one, entry_one(n)), send(kept, entry_two(n, True))
    back_x, back_window, mat_x, around, mat_y, mat_ya, k_z = mats(0)
    image = pieces(view_images, 0)
    image = send(image[0], entry_one(n)), send(image[1], entry_two(n, False)), image[1]
    main, window, part, core_low, core_high, *sent_planes = call(
        first_kernel, [field, packed, by_half, sent, sent, sent, sent], one, two, kept, mat_x, around, mat_y
    )

    for view in range(views):
        for step in range(ITERS):
            last = step + 1 == ITERS
            ahead = view + 1 < views
            if view == 0 and step == 0:
                own = call(
                    own_z_first_kernel, [piece, piece], k_z, part,
                    send(core_low, core_swap(n)), send(core_high, core_swap(n)),
                )
            else:
                own = call(own_z_both_kernel, [piece, piece], k_z, part, send(sent_core, core_swap(n)))
            chip = [send(s, chip_swap(n)) for s in sent_planes]
            if view + 1 < views and not last:
                chip[1], *next_mats = lax.optimization_barrier((chip[1], *mats(view + 1)))
            ratio, sent_core, sent_low = call(
                functools.partial(ratio_kernel, side=0), [piece, sent, sent], k_z, own[0], chip[0], *image
            )
            core_low, chip_low = send(sent_core, core_swap(n)), send(sent_low, chip_swap(n))
            chip_high, _ = lax.optimization_barrier((chip[1], ratio))
            (low,) = call(functools.partial(own_z_kernel, flip=True), [piece], k_z, ratio, core_low)
            ratio, sent_core, sent_high = call(
                functools.partial(ratio_kernel, side=1), [piece, sent, sent], k_z, own[1], chip_high, *image
            )
            core_high, chip_high = send(sent_core, core_swap(n)), send(sent_high, chip_swap(n))
            low, edge_low = call(back_edge_kernel, [piece, edge], k_z, low, chip_low, cost=10)
            edge_low = send(edge_low, half_swap(n))
            core_high, _ = lax.optimization_barrier((core_high, low))
            (high,) = call(functools.partial(own_z_kernel, flip=True), [piece], k_z, ratio, core_high)
            if ahead:
                images, _ = lax.optimization_barrier((view_images, low))
                if last:
                    next_kept, _ = lax.optimization_barrier((next_kept, low))
                    next_two = send(next_kept, entry_two(n, True))
                else:
                    next_one, next_kept = pieces(images, view + 1)
                    next_one = send(next_one, entry_one(n))
            high, edge_high = call(back_edge_kernel, [piece, edge], k_z, high, chip_high)
            edge_high = send(edge_high, half_swap(n))
            if not ahead:
                high, edge_low = lax.optimization_barrier((high, edge_low))
            if last and view + 1 == views:
                one, kept, corr = call(
                    far_last_kernel, [piece, piece, packed], low, high, main, mat_ya, back_x,
                    scratch=[pltpu.VMEM(field, F32)],
                )
                (window,) = call(
                    near_last_kernel, [edge], edge_low, edge_high, corr, window, mat_ya, back_window, cost=10
                )
                break
            old_back_x, old_back_window, old_ya = back_x, back_window, mat_ya
            if last:
                back_x, back_window, mat_x, around, mat_y, mat_ya, k_z = next_mats
            main, corr, part = call(
                far_kernel, [field, packed, field], low, high, main, old_ya, old_back_x, mat_x, mat_y, cost=1
            )
            if ahead and last:
                corr, next_two = lax.optimization_barrier((corr, next_two))
                image = next_one, next_two, next_kept
            elif ahead:
                corr, next_one = lax.optimization_barrier((corr, next_one))
            window, part, sent_core, *sent_planes = call(
                near_kernel, [packed, by_half, sent_both, sent, sent],
                edge_low, edge_high, corr, window, part, old_ya, old_back_window, mat_y, around,
            )
    (out,) = call(
        leave_kernel, [estimate_start.shape],
        send(one, back(entry_one(n))), send(kept, entry_two(n, True)), kept, send(window, entry_two(n, True)), window,
    )
    return out


def solution(mesh):
    return jax.shard_map(
        local,
        mesh=mesh,
        in_specs=(P(("grp", "gz"), "gy", None), P(None, ("grp", "gz"), "gy", None), P()),
        out_specs=P(("grp", "gz"), "gy", None),
        check_vma=False,
    )
```

```python
import functools

import jax
import jax.numpy as jnp
from jax import lax
from jax.experimental import pallas as pl
from jax.experimental.pallas import tpu as pltpu
from jax.sharding import PartitionSpec as P

ITERS = 2
AXES = ("gz", "gy")
EDGE = 32
F32, BF16 = jnp.float32, jnp.bfloat16


def spot(zp, xp, c):
    return (2 * zp + xp) * 2 + c


def core_swap(n):
    return [(spot(z, x, c), spot(z, x, 1 - c)) for z in range(n) for x in range(2) for c in range(2)]


def half_swap(n):
    return [(spot(z, x, c), spot(z, 1 - x, c)) for z in range(n) for x in range(2) for c in range(2)]


def chip_swap(n):
    pairs = []
    for x in range(2):
        for z in range(n - 1):
            pairs += [(spot(z, x, 1), spot(z + 1, x, 0)), (spot(z + 1, x, 0), spot(z, x, 1))]
        pairs += [(spot(0, x, 0), spot(0, 1 - x, 0)), (spot(n - 1, x, 1), spot(n - 1, 1 - x, 1))]
    return pairs


def entry_one(n):
    pairs = []
    for z in range(n):
        pairs += [
            (spot(z, 0, 1), spot(z, 0, 0)),
            (spot(z, 0, 0), spot(z, 1, 0)),
            (spot(z, 1, 0), spot(z, 1, 1)),
            (spot(z, 1, 1), spot(z, 0, 1)),
        ]
    return pairs


def entry_two(n, over_z):
    pairs = []
    for z in range(n):
        pairs += [(spot(z, 0, 1), spot(z, 1, 0)), (spot(z, 1, 0), spot(z, 0, 1))]
        if over_z and n % 2 == 0:
            pairs += [(spot(z, 0, 0), spot(z ^ 1, 0, 0)), (spot(z, 1, 1), spot(z ^ 1, 1, 1))]
        else:
            pairs += [(spot(z, 0, 0), spot(z, 1, 1)), (spot(z, 1, 1), spot(z, 0, 0))]
    return pairs


def back(pairs):
    return [(target, source) for source, target in pairs]


def toeplitz(row, half):
    size = row.shape[1]
    base = pltpu.roll(jnp.broadcast_to(row, (size, size)), size - half, 1)
    return pltpu.roll(base, 0, 1, stride=1, stride_axis=0)


def taps_row(taps_ref, view, axis, row_ref):
    taps = taps_ref.shape[2]
    row_ref[...] = jnp.zeros(row_ref.shape, F32)
    row_ref[:, :taps] = taps_ref[view, axis : axis + 1, :]
    row = row_ref[...]
    return row / jnp.sum(row, axis=1, keepdims=True)


def put_halves(ref, matrix):
    ref[0], ref[1] = split(matrix)


def lanes(shape, axis):
    return lax.broadcasted_iota(jnp.int32, shape, axis)


def split(value):
    high = value.astype(BF16)
    return high, (value - high.astype(F32)).astype(BF16)


def dot(a, b):
    return jnp.dot(a, b, preferred_element_type=F32)


def times_right(value, mat_ref):
    high, low = split(value)
    return dot(high, mat_ref[0]) + (dot(low, mat_ref[0]) + dot(high, mat_ref[1]))


def times_left(mat_ref, value):
    high, low = split(value)
    return dot(mat_ref[0], high) + (dot(mat_ref[0], low) + dot(mat_ref[1], high))


def call(kernel, outs, *args, scratch=(), cost=0):
    def spec(a):
        small = a.ndim == 1
        return pl.BlockSpec(memory_space=pltpu.SMEM if small else pltpu.VMEM)

    return pl.pallas_call(
        kernel,
        out_shape=[jax.ShapeDtypeStruct(s, F32) if isinstance(s, tuple) else s for s in outs],
        in_specs=[spec(a) for a in args],
        out_specs=[pl.BlockSpec(memory_space=pltpu.VMEM) for _ in outs],
        scratch_shapes=list(scratch),
        compiler_params=pltpu.CompilerParams(vmem_limit_bytes=24 * 1024 * 1024),
        cost_estimate=pl.CostEstimate(flops=1 + cost * 10**9, bytes_accessed=1 + cost * 3 * 10**6, transcendentals=0),
    )(*args)


def place():
    core, gz, n = lax.axis_index("gy"), lax.axis_index("gz"), lax.axis_size("gz") // 2
    at_end = ((gz < 2) & (core == 0)) | ((gz >= 2 * n - 2) & (core == 1))
    return core, gz % 2, jnp.where(at_end, 0, 1)


def cut_kernel(est_ref, one_ref, two_ref):
    planes, rows, cols = est_ref.shape
    wide = cols // 2
    groups = wide // EDGE
    each = planes // groups
    lower = place()[0] == 0
    packed = None
    for g in range(groups):
        at = slice(each * g, each * (g + 1))
        block = est_ref[at].reshape(each * rows, cols)
        low, high = block[:, :wide].reshape(each, rows, wide), block[:, wide:].reshape(each, rows, wide)
        one_ref[at] = jnp.where(lower, high, low)
        two_ref[at] = jnp.where(lower, low, high)
        turned = pltpu.roll(block, (EDGE * g - wide + EDGE // 2) % cols, 1)[:, :wide]
        packed = turned if packed is None else jnp.where(lanes(turned.shape, 1) // EDGE == g, turned, packed)
    packed = packed.reshape(each, rows, wide)
    one_ref[planes:] = packed
    two_ref[planes:] = packed


def first_kernel(
    one_ref, two_ref, kept_ref, mat_x, mat_around, mat_y,
    main_out, window_out, part_out, core_low_ref, core_high_ref, low_ref, high_ref,
):
    planes, rows, cols = main_out.shape
    half = rows // 2
    first = place()[1] == 0

    one, two = one_ref[...], jnp.where(stays(), kept_ref[...], two_ref[...])
    low, high = jnp.where(first, two, one), jnp.where(first, one, two)
    main_out[:, :half], main_out[:, half:] = low[:planes], high[:planes]
    groups = cols // EDGE
    each = planes // groups
    size = each * rows
    window = jnp.concatenate([low[planes:], high[planes:]], axis=1).reshape(size, cols)
    window_out[...] = window
    for pair in range(groups // 2):
        both = (2 * pair, 2 * pair + 1)
        blocks = [main_out[each * g : each * (g + 1)].reshape(size, cols) for g in both]
        part = jnp.concatenate([times_right(block, mat_x) for block in blocks], axis=1)
        part = times_left(mat_y, part + times_right(window, mat_around.at[pair]))
        for side, g in enumerate(both):
            put_rows(
                part_out, slice(each * g, each * (g + 1)),
                part[:, cols * side : cols * (side + 1)].reshape(each, rows, cols),
            )
    put_sent(part_out, (core_low_ref, core_high_ref), low_ref, high_ref)


def stays():
    core, xp, _ = place()
    return core == xp


def put_rows(out_ref, at, block):
    rows = out_ref.shape[2]
    out_ref[0, at], out_ref[1, at] = block[:, :rows], block[:, rows:]


def put_sent(out_ref, core_ref, low_ref, high_ref):
    flags = place()
    sent = low_ref.shape[0]
    spare = out_ref.shape[1] - sent
    at = pl.ds((1 - flags[0]) * spare, sent)
    core_ref[0][...], core_ref[1][...] = out_ref[0, at], out_ref[1, at]
    at = pl.ds(flags[0] * spare, sent)
    low_ref[...], high_ref[...] = out_ref[0, at], out_ref[1, at]


def pack_edge(blocks):
    first = jnp.where(place()[1] == 0, EDGE, 0)
    packed = None
    for g, block in enumerate(blocks):
        cols = block.shape[1]
        turned = pltpu.roll(block, (EDGE * g + first) % cols, 1)
        if packed is None:
            packed = turned
        else:
            lane = lax.broadcasted_iota(jnp.int32, block.shape, 1)
            packed = jnp.where(lane // EDGE == g, turned, packed)
    return packed


def mats_kernel(
    taps_ref, back_x_ref, back_window_ref, x_ref, window_ref, y_ref, ya_ref, z_ref,
    full, turned, row_ref, *, view, rows
):
    size, wide = full.shape[0], x_ref.shape[1]
    taps = z_ref.shape[0]
    groups = wide // EDGE
    near = EDGE // 2
    flags = place()
    first = flags[1] == 0
    diff = lanes((size, size), 0) - lanes((size, size), 1)
    band_x = jnp.where(jnp.abs(diff) <= taps // 2, toeplitz(taps_row(taps_ref, view, 2, row_ref), taps // 2), 0.0)
    full[...] = band_x
    turned[...] = band_x.T
    main = pl.ds(pl.multiple_of(flags[1] * wide, wide), wide)
    here = full[main, :]
    block = jnp.where(first, here[:, :wide], here[:, wide:])
    lane = lanes((wide, wide), 1)
    for g in range(groups):
        moved = pltpu.roll(here, (EDGE * g - wide + near) % size, 1)[:, :wide]
        moved = jnp.where(lane // EDGE == g, moved, 0.0)
        put_halves(back_x_ref.at[g], jnp.concatenate([block, moved], axis=1))
    beyond = full[pl.ds(pl.multiple_of(jnp.where(first, wide, wide - EDGE), EDGE), EDGE), :]
    parts = []
    for g in range(groups):
        moved = pltpu.roll(beyond, (EDGE * g - wide + near) % size, 1)[:, :wide]
        parts.append(jnp.where(lanes((EDGE, wide), 1) // EDGE == g, moved, 0.0))
    put_halves(back_window_ref, jnp.concatenate(parts, axis=0))
    here = turned[main, :]
    block = jnp.where(first, here[:, :wide], here[:, wide:])
    row = lanes((wide, wide), 0)
    apart = jnp.where(first, row, row - near)
    put_halves(x_ref, jnp.where((apart >= 0) & (apart < wide - near), block, 0.0))
    around = turned[wide - near : wide + near, :]
    around = jnp.where(first, around[:, :wide], around[:, wide:])
    zero = jnp.zeros((EDGE, wide), F32)
    for pair in range(groups // 2):
        both = [
            jnp.concatenate([around if g == 2 * pair + side else zero for g in range(groups)], axis=0)
            for side in range(2)
        ]
        put_halves(window_ref.at[pair], jnp.concatenate(both, axis=1))
    band_y = toeplitz(taps_row(taps_ref, view, 1, row_ref), taps // 2)
    band_y = jnp.where(lanes((size, size), 0) // rows == lanes((size, size), 1) // rows, band_y, 0.0)
    put_halves(y_ref, band_y)
    put_halves(ya_ref, band_y.T)
    line = taps_row(taps_ref, view, 0, row_ref)
    for tap in range(taps):
        z_ref[tap] = jnp.broadcast_to(line[:, tap : tap + 1], z_ref.shape[1:])


def add_planes(total, taps_ref, field, flip):
    taps = taps_ref.shape[0]
    half = taps // 2
    for tap in range(taps):
        weight = None
        for i in range(len(total)):
            plane = field.get(i + tap - half)
            if plane is None:
                continue
            if weight is None:
                weight = taps_ref[taps - 1 - tap if flip else tap]
            term = weight * plane
            total[i] = term if total[i] is None else total[i] + term
    return total


def own_z_kernel(taps, own_ref, core_ref, out_ref, *, flip):
    parts, planes, rows, _ = own_ref.shape
    flags = place()
    half = taps.shape[0] // 2
    tiles = rows // 8
    for core in range(2):

        @pl.when(flags[0] == core)
        def _():
            def step(i, carry):
                part, at = i // tiles, pl.ds(pl.multiple_of(i % tiles * 8, 8), 8)
                field = {j: own_ref[part, j, at, :] for j in range(planes)}
                for j in range(half):
                    field[planes + j if core == 0 else j - half] = core_ref[part, j, at, :]
                total = add_planes([None] * planes, taps, field, flip)
                for j in range(planes):
                    out_ref[part, j, at, :] = total[j]
                return carry

            lax.fori_loop(0, parts * tiles, step, 0)


def own_z_half_kernel(taps, own_ref, core_ref, out_ref):
    grown = (1, *own_ref.shape)
    own_z_kernel(taps, own_ref.reshape(grown), core_ref.reshape(1, *core_ref.shape), out_ref.reshape(grown), flip=True)


def own_z_first_kernel(taps, own_ref, core_low_ref, core_high_ref, out_ref, core_ref):
    core_ref[0], core_ref[1] = core_low_ref[...], core_high_ref[...]
    own_z_kernel(taps, own_ref, core_ref, out_ref, flip=False)


def finish_z(taps, part_ref, chip_ref, flip, put):
    planes, rows, _ = part_ref.shape
    half = chip_ref.shape[0]
    flags = place()
    for case in range(3):
        wanted = (flags[2] == 0) if case == 2 else (flags[2] == 1) & (flags[0] == case)

        @pl.when(wanted)
        def _():
            def step(i, carry):
                at = pl.ds(pl.multiple_of(i * 8, 8), 8)
                total = [part_ref[j, at, :] for j in range(planes)]
                if case < 2:
                    first = -half if case == 0 else planes
                    field = {first + j: chip_ref[j, at, :] for j in range(half)}
                    total = add_planes(total, taps, field, flip)
                put(at, total)
                return carry

            lax.fori_loop(0, rows // 8, step, 0)


def ratio_kernel(taps, part_ref, chip_ref, one_ref, two_ref, kept_ref, out_ref, core_ref, send_ref, *, side):
    planes = part_ref.shape[1]
    flags = place()
    from_two, keep = flags[1] == side, stays()

    def put(at, blurred):
        for j in range(planes):
            two = jnp.where(keep, kept_ref[j, at, :], two_ref[j, at, :])
            out_ref[j, at, :] = jnp.where(from_two, two, one_ref[j, at, :]) / blurred[j]

    finish_z(taps, part_ref.at[side], chip_ref, False, put)
    sent = send_ref.shape[0]
    core_ref[...] = out_ref[pl.ds((1 - flags[0]) * (planes - sent), sent)]
    send_ref[...] = out_ref[pl.ds(flags[0] * (planes - sent), sent)]


def back_kernel(taps, part_ref, chip_ref, out_ref):
    def put(at, total):
        for j in range(len(total)):
            out_ref[j, at, :] = total[j]

    finish_z(taps, part_ref, chip_ref, True, put)


def joined_rows(low_ref, high_ref, at):
    block = jnp.concatenate([low_ref[at], high_ref[at]], axis=1)
    return block.reshape(block.shape[0] * block.shape[1], block.shape[2])


def back_edge_kernel(taps, part_ref, chip_ref, out_ref, edge_ref):
    back_kernel(taps, part_ref, chip_ref, out_ref)
    planes, rows, cols = out_ref.shape
    groups = cols // EDGE
    each = planes // groups
    packed = pack_edge([out_ref[each * g : each * (g + 1)].reshape(each * rows, cols) for g in range(groups)])
    edge_ref[...] = packed.reshape(edge_ref.shape)


def far_kernel(low_ref, high_ref, est_ref, mat_ya, mat_xa, mat_x, mat_y, est_out, corr_out, part_out):
    planes, rows, cols = est_ref.shape
    groups = cols // EDGE
    each = planes // groups
    size = each * rows
    corr_out[...] = jnp.zeros(corr_out.shape, F32)

    def step(pair, carry):
        both = [(2 * pair + side, pl.ds(each * (2 * pair + side), each)) for side in range(2)]
        block = jnp.concatenate([joined_rows(low_ref, high_ref, at) for _, at in both], axis=1)
        block = times_left(mat_ya, block)
        wide = []
        for side, (g, at) in enumerate(both):
            corr = times_right(block[:, cols * side : cols * (side + 1)], mat_xa.at[g])
            corr_out[...] += corr[:, cols:]
            est = est_ref[at].reshape(size, cols) * corr[:, :cols]
            est_out[at] = est.reshape(each, rows, cols)
            if part_out is not None:
                wide.append(times_right(est, mat_x))
        if part_out is not None:
            part = times_left(mat_y, jnp.concatenate(wide, axis=1))
            for side, (_, at) in enumerate(both):
                part_out[at] = part[:, cols * side : cols * (side + 1)].reshape(each, rows, cols)
        return carry

    lax.fori_loop(0, groups // 2, step, 0)


def far_last_kernel(low_ref, high_ref, est_ref, mat_ya, mat_xa, one_out, two_out, corr_out, est):
    far_kernel(low_ref, high_ref, est_ref, mat_ya, mat_xa, None, None, est, corr_out, None)
    half = est.shape[1] // 2
    first = place()[1] == 0
    low, high = est[:, :half], est[:, half:]
    one_out[...] = jnp.where(first, high, low)
    two_out[...] = jnp.where(first, low, high)


def near_window(edge_low, edge_high, corr_ref, window_ref, mat_ya, mat_window):
    edge = times_left(mat_ya, joined_rows(edge_low, edge_high, slice(None)))
    return window_ref[...] * (corr_ref[...] + times_right(edge, mat_window))


def near_kernel(
    edge_low, edge_high, corr_ref, window_ref, part_ref, mat_ya, mat_window, mat_y, mat_around,
    window_out, part_out, core_ref, low_ref, high_ref,
):
    planes, rows, cols = part_ref.shape
    groups = cols // EDGE
    each = planes // groups
    window = near_window(edge_low, edge_high, corr_ref, window_ref, mat_ya, mat_window)
    window_out[...] = window
    blurred = times_left(mat_y, window)

    def step(pair, carry):
        share = times_right(blurred, mat_around.at[pair])
        for side in range(2):
            at = pl.ds(each * (2 * pair + side), each)
            put_rows(
                part_out, at, part_ref[at] + share[:, cols * side : cols * (side + 1)].reshape(each, rows, cols)
            )
        return carry

    lax.fori_loop(0, groups // 2, step, 0)
    put_sent(part_out, (core_ref.at[0], core_ref.at[1]), low_ref, high_ref)


def near_last_kernel(edge_low, edge_high, corr_ref, window_ref, mat_ya, mat_window, out_ref):
    window = near_window(edge_low, edge_high, corr_ref, window_ref, mat_ya, mat_window)
    each, half, cols = out_ref.shape
    window = window.reshape(each, 2 * half, cols)
    out_ref[...] = jnp.where(place()[1] == 0, window[:, :half], window[:, half:])


def leave_kernel(one_ref, two_ref, kept_ref, window_ref, window_kept_ref, out_ref):
    planes, rows, wide = one_ref.shape
    groups = wide // EDGE
    each = planes // groups
    lower = place()[0] == 0
    one, two = one_ref[...], jnp.where(stays(), kept_ref[...], two_ref[...])
    window = jnp.where(stays(), window_kept_ref[...], window_ref[...]).reshape(each * rows, wide)
    window = jnp.concatenate([window, window], axis=1)
    from_cut = lanes(window.shape, 1) - wide + EDGE // 2
    for g in range(groups):
        at = slice(each * g, each * (g + 1))
        block = jnp.concatenate([jnp.where(lower, two[at], one[at]), jnp.where(lower, one[at], two[at])], axis=2)
        turned = pltpu.roll(window, (wide - EDGE // 2 - EDGE * g) % (2 * wide), 1)
        block = jnp.where((from_cut >= 0) & (from_cut < EDGE), turned, block.reshape(each * rows, 2 * wide))
        out_ref[at] = block.reshape(each, rows, 2 * wide)


def local(estimate_start, view_images, psf_taps):
    planes, rows_dev, cols = estimate_start.shape
    views, _, taps = psf_taps.shape
    half = taps // 2
    n = lax.axis_size("gz") // 2
    rows, wide = rows_dev * lax.axis_size("gy"), cols // 2
    core = lax.axis_index("gy")
    send = lambda value, pairs: lax.ppermute(value, AXES, pairs)
    groups = wide // EDGE
    rows_y = planes * rows // groups
    field, packed, piece = (planes, rows, wide), (rows_y, wide), (planes, rows_dev, wide)
    sent, by_half = (half, rows_dev, wide), (2, *piece)
    sent_both, edge = (2, *sent), (planes // groups, rows_dev, wide)

    def mats(view):
        pair = lambda *shape: jax.ShapeDtypeStruct(shape, BF16)
        return call(
            functools.partial(mats_kernel, view=view, rows=rows),
            [
                pair(groups, 2, wide, 2 * wide),
                pair(2, wide, wide),
                pair(2, wide, wide),
                pair(groups // 2, 2, wide, 2 * wide),
                pair(2, rows_y, rows_y),
                pair(2, rows_y, rows_y),
                (taps, 8, wide),
            ],
            psf_taps, scratch=[pltpu.VMEM((cols, cols), F32)] * 2 + [pltpu.VMEM((1, cols), F32)],
        )

    def pieces(value, *index):
        def cut(half):
            start = (*index, 0, 0, wide * half)
            return lax.dynamic_slice(value, start, (1,) * len(index) + piece).reshape(piece)

        return cut(1 - core), cut(core)

    entry = (planes + planes // groups, rows_dev, wide)
    one, kept = call(cut_kernel, [entry, entry], estimate_start)
    one, two = send(one, entry_one(n)), send(kept, entry_two(n, True))
    back_x, back_window, mat_x, around, mat_y, mat_ya, k_z = mats(0)
    image = pieces(view_images, 0)
    image = send(image[0], entry_one(n)), send(image[1], entry_two(n, False)), image[1]
    main, window, part, core_low, core_high, *sent_planes = call(
        first_kernel, [field, packed, by_half, sent, sent, sent, sent], one, two, kept, mat_x, around, mat_y
    )

    for view in range(views):
        for step in range(ITERS):
            last = step + 1 == ITERS
            ahead = view + 1 < views
            if ahead and not last:
                images, _ = lax.optimization_barrier((view_images, part))
                next_pieces = pieces(images, view + 1)
            if view == 0 and step == 0:
                (own,) = call(
                    own_z_first_kernel, [by_half], k_z, part,
                    send(core_low, core_swap(n)), send(core_high, core_swap(n)), scratch=[pltpu.VMEM(sent_both, F32)],
                )
            else:
                (own,) = call(
                    functools.partial(own_z_kernel, flip=False), [by_half], k_z, part, send(sent_core, core_swap(n))
                )
            chip = [send(s, chip_swap(n)) for s in sent_planes]
            if view + 1 < views and not last:
                chip[1], *next_mats = lax.optimization_barrier((chip[1], *mats(view + 1)))
            ratio, sent_core, sent_low = call(
                functools.partial(ratio_kernel, side=0), [piece, sent, sent], k_z, own, chip[0], *image
            )
            core_low, chip_low = send(sent_core, core_swap(n)), send(sent_low, chip_swap(n))
            chip_high, _ = lax.optimization_barrier((chip[1], ratio))
            (low,) = call(own_z_half_kernel, [piece], k_z, ratio, core_low)
            ratio, sent_core, sent_high = call(
                functools.partial(ratio_kernel, side=1), [piece, sent, sent], k_z, own, chip_high, *image
            )
            core_high, chip_high = send(sent_core, core_swap(n)), send(sent_high, chip_swap(n))
            low, edge_low = call(back_edge_kernel, [piece, edge], k_z, low, chip_low, cost=10)
            edge_low = send(edge_low, half_swap(n))
            core_high, _ = lax.optimization_barrier((core_high, low))
            (high,) = call(own_z_half_kernel, [piece], k_z, ratio, core_high)
            if ahead:
                if last:
                    next_kept, _ = lax.optimization_barrier((next_kept, low))
                    next_two = send(next_kept, entry_two(n, True))
                else:
                    next_one, next_kept, _ = lax.optimization_barrier((*next_pieces, low))
                    next_one = send(next_one, entry_one(n))
            high, edge_high = call(back_edge_kernel, [piece, edge], k_z, high, chip_high)
            edge_high = send(edge_high, half_swap(n))
            if not ahead:
                high, edge_low = lax.optimization_barrier((high, edge_low))
            if last and view + 1 == views:
                one, kept, corr = call(
                    far_last_kernel, [piece, piece, packed], low, high, main, mat_ya, back_x,
                    scratch=[pltpu.VMEM(field, F32)],
                )
                (window,) = call(
                    near_last_kernel, [edge], edge_low, edge_high, corr, window, mat_ya, back_window, cost=10
                )
                break
            old_back_x, old_back_window, old_ya = back_x, back_window, mat_ya
            if last:
                back_x, back_window, mat_x, around, mat_y, mat_ya, k_z = next_mats
            main, corr, part = call(
                far_kernel, [field, packed, field], low, high, main, old_ya, old_back_x, mat_x, mat_y, cost=1
            )
            if ahead and last:
                corr, next_two = lax.optimization_barrier((corr, next_two))
                image = next_one, next_two, next_kept
            elif ahead:
                corr, next_one = lax.optimization_barrier((corr, next_one))
            window, part, sent_core, *sent_planes = call(
                near_kernel, [packed, by_half, sent_both, sent, sent],
                edge_low, edge_high, corr, window, part, old_ya, old_back_window, mat_y, around,
            )
    (out,) = call(
        leave_kernel, [estimate_start.shape],
        send(one, back(entry_one(n))), send(kept, entry_two(n, True)), kept, send(window, entry_two(n, True)), window,
    )
    return out


def solution(mesh):
    return jax.shard_map(
        local,
        mesh=mesh,
        in_specs=(P(("grp", "gz"), "gy", None), P(None, ("grp", "gz"), "gy", None), P()),
        out_specs=P(("grp", "gz"), "gy", None),
        check_vma=False,
    )
```

```python
import functools

import jax
import jax.numpy as jnp
from jax import lax
from jax.experimental import pallas as pl
from jax.experimental.pallas import tpu as pltpu
from jax.sharding import PartitionSpec as P

ITERS = 2
AXES = ("gz", "gy")
EDGE = 32
F32, BF16 = jnp.float32, jnp.bfloat16


def spot(zp, xp, c):
    return (2 * zp + xp) * 2 + c


def core_swap(n):
    return [(spot(z, x, c), spot(z, x, 1 - c)) for z in range(n) for x in range(2) for c in range(2)]


def half_swap(n):
    return [(spot(z, x, c), spot(z, 1 - x, c)) for z in range(n) for x in range(2) for c in range(2)]


def chip_swap(n):
    pairs = []
    for x in range(2):
        for z in range(n - 1):
            pairs += [(spot(z, x, 1), spot(z + 1, x, 0)), (spot(z + 1, x, 0), spot(z, x, 1))]
        pairs += [(spot(0, x, 0), spot(0, 1 - x, 0)), (spot(n - 1, x, 1), spot(n - 1, 1 - x, 1))]
    return pairs


def entry_one(n):
    pairs = []
    for z in range(n):
        pairs += [
            (spot(z, 0, 1), spot(z, 0, 0)),
            (spot(z, 0, 0), spot(z, 1, 0)),
            (spot(z, 1, 0), spot(z, 1, 1)),
            (spot(z, 1, 1), spot(z, 0, 1)),
        ]
    return pairs


def entry_two(n, over_z):
    pairs = []
    for z in range(n):
        pairs += [(spot(z, 0, 1), spot(z, 1, 0)), (spot(z, 1, 0), spot(z, 0, 1))]
        if over_z and n % 2 == 0:
            pairs += [(spot(z, 0, 0), spot(z ^ 1, 0, 0)), (spot(z, 1, 1), spot(z ^ 1, 1, 1))]
        else:
            pairs += [(spot(z, 0, 0), spot(z, 1, 1)), (spot(z, 1, 1), spot(z, 0, 0))]
    return pairs


def back(pairs):
    return [(target, source) for source, target in pairs]


def toeplitz(row, half):
    size = row.shape[1]
    base = pltpu.roll(jnp.broadcast_to(row, (size, size)), size - half, 1)
    return pltpu.roll(base, 0, 1, stride=1, stride_axis=0)


def taps_row(taps_ref, view, axis, row_ref):
    taps = taps_ref.shape[2]
    row_ref[...] = jnp.zeros(row_ref.shape, F32)
    row_ref[:, :taps] = taps_ref[view, axis : axis + 1, :]
    row = row_ref[...]
    return row / jnp.sum(row, axis=1, keepdims=True)


def put_halves(ref, matrix):
    ref[0], ref[1] = split(matrix)


def lanes(shape, axis):
    return lax.broadcasted_iota(jnp.int32, shape, axis)


def split(value):
    high = value.astype(BF16)
    return high, (value - high.astype(F32)).astype(BF16)


def dot(a, b):
    return jnp.dot(a, b, preferred_element_type=F32)


def times_right(value, mat_ref):
    high, low = split(value)
    if value.shape[1] >= 256:
        return dot(high, mat_ref[0]) + (dot(low, mat_ref[0]) + dot(high, mat_ref[1]))
    twice = jnp.concatenate([mat_ref[0], mat_ref[0]], axis=0)
    return dot(jnp.concatenate([high, low], axis=1), twice) + dot(high, mat_ref[1])


def times_left(mat_ref, value):
    high, low = split(value)
    cols = value.shape[1]
    if cols >= 256:
        return dot(mat_ref[0], high) + (dot(mat_ref[0], low) + dot(mat_ref[1], high))
    both = dot(mat_ref[0], jnp.concatenate([high, low], axis=1))
    return both[:, :cols] + (both[:, cols:] + dot(mat_ref[1], high))


def call(kernel, outs, *args, scratch=(), cost=0):
    def spec(a):
        small = a.ndim == 1
        return pl.BlockSpec(memory_space=pltpu.SMEM if small else pltpu.VMEM)

    return pl.pallas_call(
        kernel,
        out_shape=[jax.ShapeDtypeStruct(s, F32) if isinstance(s, tuple) else s for s in outs],
        in_specs=[spec(a) for a in args],
        out_specs=[pl.BlockSpec(memory_space=pltpu.VMEM) for _ in outs],
        scratch_shapes=list(scratch),
        compiler_params=pltpu.CompilerParams(vmem_limit_bytes=24 * 1024 * 1024),
        cost_estimate=pl.CostEstimate(flops=1 + cost * 10**9, bytes_accessed=1 + cost * 3 * 10**6, transcendentals=0),
    )(*args)


def place():
    core, gz, n = lax.axis_index("gy"), lax.axis_index("gz"), lax.axis_size("gz") // 2
    at_end = ((gz < 2) & (core == 0)) | ((gz >= 2 * n - 2) & (core == 1))
    return core, gz % 2, jnp.where(at_end, 0, 1)


def cut_kernel(est_ref, one_ref, two_ref):
    planes, rows, cols = est_ref.shape
    wide = cols // 2
    groups = wide // EDGE
    each = planes // groups
    lower = place()[0] == 0
    packed = None
    for g in range(groups):
        at = slice(each * g, each * (g + 1))
        block = est_ref[at].reshape(each * rows, cols)
        low, high = block[:, :wide].reshape(each, rows, wide), block[:, wide:].reshape(each, rows, wide)
        one_ref[at] = jnp.where(lower, high, low)
        two_ref[at] = jnp.where(lower, low, high)
        turned = pltpu.roll(block, (EDGE * g - wide + EDGE // 2) % cols, 1)[:, :wide]
        packed = turned if packed is None else jnp.where(lanes(turned.shape, 1) // EDGE == g, turned, packed)
    packed = packed.reshape(each, rows, wide)
    one_ref[planes:] = packed
    two_ref[planes:] = packed


def first_kernel(
    one_ref, two_ref, kept_ref, mat_x, mat_around, mat_y,
    main_out, window_out, part_out, core_low_ref, core_high_ref, low_ref, high_ref,
):
    planes, rows, cols = main_out.shape
    half = rows // 2
    first = place()[1] == 0

    one, two = one_ref[...], jnp.where(stays(), kept_ref[...], two_ref[...])
    low, high = jnp.where(first, two, one), jnp.where(first, one, two)
    main_out[:, :half], main_out[:, half:] = low[:planes], high[:planes]
    groups = cols // EDGE
    each = planes // groups
    size = each * rows
    window = jnp.concatenate([low[planes:], high[planes:]], axis=1).reshape(size, cols)
    window_out[...] = window
    for pair in range(groups // 2):
        both = (2 * pair, 2 * pair + 1)
        blocks = [main_out[each * g : each * (g + 1)].reshape(size, cols) for g in both]
        part = jnp.concatenate([times_right(block, mat_x) for block in blocks], axis=1)
        part = times_left(mat_y, part + times_right(window, mat_around.at[pair]))
        for side, g in enumerate(both):
            put_rows(
                part_out, slice(each * g, each * (g + 1)),
                part[:, cols * side : cols * (side + 1)].reshape(each, rows, cols),
            )
    put_sent(part_out, (core_low_ref, core_high_ref), low_ref, high_ref)


def stays():
    core, xp, _ = place()
    return core == xp


def put_rows(out_ref, at, block):
    rows = out_ref.shape[2]
    out_ref[0, at], out_ref[1, at] = block[:, :rows], block[:, rows:]


def put_sent(out_ref, core_ref, low_ref, high_ref):
    flags = place()
    sent = low_ref.shape[0]
    spare = out_ref.shape[1] - sent
    at = pl.ds((1 - flags[0]) * spare, sent)
    core_ref[0][...], core_ref[1][...] = out_ref[0, at], out_ref[1, at]
    at = pl.ds(flags[0] * spare, sent)
    low_ref[...], high_ref[...] = out_ref[0, at], out_ref[1, at]


def pack_edge(blocks):
    first = jnp.where(place()[1] == 0, EDGE, 0)
    packed = None
    for g, block in enumerate(blocks):
        cols = block.shape[1]
        turned = pltpu.roll(block, (EDGE * g + first) % cols, 1)
        if packed is None:
            packed = turned
        else:
            lane = lax.broadcasted_iota(jnp.int32, block.shape, 1)
            packed = jnp.where(lane // EDGE == g, turned, packed)
    return packed


def mats_kernel(
    taps_ref, back_x_ref, back_window_ref, x_ref, window_ref, y_ref, ya_ref, z_ref,
    full, turned, row_ref, *, view, rows
):
    size, wide = full.shape[0], x_ref.shape[1]
    taps = z_ref.shape[0]
    groups = wide // EDGE
    near = EDGE // 2
    flags = place()
    first = flags[1] == 0
    diff = lanes((size, size), 0) - lanes((size, size), 1)
    band_x = jnp.where(jnp.abs(diff) <= taps // 2, toeplitz(taps_row(taps_ref, view, 2, row_ref), taps // 2), 0.0)
    full[...] = band_x
    turned[...] = band_x.T
    main = pl.ds(pl.multiple_of(flags[1] * wide, wide), wide)
    here = full[main, :]
    block = jnp.where(first, here[:, :wide], here[:, wide:])
    lane = lanes((wide, wide), 1)
    for g in range(groups):
        moved = pltpu.roll(here, (EDGE * g - wide + near) % size, 1)[:, :wide]
        moved = jnp.where(lane // EDGE == g, moved, 0.0)
        put_halves(back_x_ref.at[g], jnp.concatenate([block, moved], axis=1))
    beyond = full[pl.ds(pl.multiple_of(jnp.where(first, wide, wide - EDGE), EDGE), EDGE), :]
    parts = []
    for g in range(groups):
        moved = pltpu.roll(beyond, (EDGE * g - wide + near) % size, 1)[:, :wide]
        parts.append(jnp.where(lanes((EDGE, wide), 1) // EDGE == g, moved, 0.0))
    put_halves(back_window_ref, jnp.concatenate(parts, axis=0))
    here = turned[main, :]
    block = jnp.where(first, here[:, :wide], here[:, wide:])
    row = lanes((wide, wide), 0)
    apart = jnp.where(first, row, row - near)
    put_halves(x_ref, jnp.where((apart >= 0) & (apart < wide - near), block, 0.0))
    around = turned[wide - near : wide + near, :]
    around = jnp.where(first, around[:, :wide], around[:, wide:])
    zero = jnp.zeros((EDGE, wide), F32)
    for pair in range(groups // 2):
        both = [
            jnp.concatenate([around if g == 2 * pair + side else zero for g in range(groups)], axis=0)
            for side in range(2)
        ]
        put_halves(window_ref.at[pair], jnp.concatenate(both, axis=1))
    band_y = toeplitz(taps_row(taps_ref, view, 1, row_ref), taps // 2)
    band_y = jnp.where(lanes((size, size), 0) // rows == lanes((size, size), 1) // rows, band_y, 0.0)
    put_halves(y_ref, band_y)
    put_halves(ya_ref, band_y.T)
    line = taps_row(taps_ref, view, 0, row_ref)
    for tap in range(taps):
        z_ref[tap] = jnp.broadcast_to(line[:, tap : tap + 1], z_ref.shape[1:])


def add_planes(total, taps_ref, field, flip):
    taps = taps_ref.shape[0]
    half = taps // 2
    for tap in range(taps):
        weight = None
        for i in range(len(total)):
            plane = field.get(i + tap - half)
            if plane is None:
                continue
            if weight is None:
                weight = taps_ref[taps - 1 - tap if flip else tap]
            term = weight * plane
            total[i] = term if total[i] is None else total[i] + term
    return total


def own_z_kernel(taps, own_ref, core_ref, out_ref, *, flip):
    parts, planes, rows, _ = own_ref.shape
    flags = place()
    half = taps.shape[0] // 2
    tiles = rows // 8
    for core in range(2):

        @pl.when(flags[0] == core)
        def _():
            def step(i, carry):
                part, at = i // tiles, pl.ds(pl.multiple_of(i % tiles * 8, 8), 8)
                field = {j: own_ref[part, j, at, :] for j in range(planes)}
                for j in range(half):
                    field[planes + j if core == 0 else j - half] = core_ref[part, j, at, :]
                total = add_planes([None] * planes, taps, field, flip)
                for j in range(planes):
                    out_ref[part, j, at, :] = total[j]
                return carry

            lax.fori_loop(0, parts * tiles, step, 0)


def own_z_mats_kernel(taps, own_ref, core_ref, psf_ref, out_ref, *refs, view, rows):
    own_z_kernel(taps, own_ref, core_ref, out_ref, flip=False)
    mats_kernel(psf_ref, *refs, view=view, rows=rows)


def own_z_first_mats_kernel(taps, own_ref, core_low_ref, core_high_ref, psf_ref, out_ref, *refs, view, rows):
    *refs, core_ref = refs
    own_z_first_kernel(taps, own_ref, core_low_ref, core_high_ref, out_ref, core_ref)
    mats_kernel(psf_ref, *refs, view=view, rows=rows)


def own_z_half_kernel(taps, own_ref, core_ref, out_ref):
    grown = (1, *own_ref.shape)
    own_z_kernel(taps, own_ref.reshape(grown), core_ref.reshape(1, *core_ref.shape), out_ref.reshape(grown), flip=True)


def own_z_first_kernel(taps, own_ref, core_low_ref, core_high_ref, out_ref, core_ref):
    core_ref[0], core_ref[1] = core_low_ref[...], core_high_ref[...]
    own_z_kernel(taps, own_ref, core_ref, out_ref, flip=False)


def finish_z(taps, part_ref, chip_ref, flip, put):
    planes, rows, _ = part_ref.shape
    half = chip_ref.shape[0]
    flags = place()
    for case in range(3):
        wanted = (flags[2] == 0) if case == 2 else (flags[2] == 1) & (flags[0] == case)

        @pl.when(wanted)
        def _():
            def step(i, carry):
                at = pl.ds(pl.multiple_of(i * 8, 8), 8)
                total = [part_ref[j, at, :] for j in range(planes)]
                if case < 2:
                    first = -half if case == 0 else planes
                    field = {first + j: chip_ref[j, at, :] for j in range(half)}
                    total = add_planes(total, taps, field, flip)
                put(at, total)
                return carry

            lax.fori_loop(0, rows // 8, step, 0)


def ratio_kernel(taps, part_ref, chip_ref, one_ref, two_ref, kept_ref, out_ref, core_ref, send_ref, *, side):
    planes = part_ref.shape[1]
    flags = place()
    from_two, keep = flags[1] == side, stays()

    def put(at, blurred):
        for j in range(planes):
            two = jnp.where(keep, kept_ref[j, at, :], two_ref[j, at, :])
            out_ref[j, at, :] = jnp.where(from_two, two, one_ref[j, at, :]) / blurred[j]

    finish_z(taps, part_ref.at[side], chip_ref, False, put)
    sent = send_ref.shape[0]
    core_ref[...] = out_ref[pl.ds((1 - flags[0]) * (planes - sent), sent)]
    send_ref[...] = out_ref[pl.ds(flags[0] * (planes - sent), sent)]


def back_kernel(taps, part_ref, chip_ref, out_ref):
    def put(at, total):
        for j in range(len(total)):
            out_ref[j, at, :] = total[j]

    finish_z(taps, part_ref, chip_ref, True, put)


def joined_rows(low_ref, high_ref, at):
    block = jnp.concatenate([low_ref[at], high_ref[at]], axis=1)
    return block.reshape(block.shape[0] * block.shape[1], block.shape[2])


def back_edge_kernel(taps, part_ref, chip_ref, out_ref, edge_ref):
    back_kernel(taps, part_ref, chip_ref, out_ref)
    planes, rows, cols = out_ref.shape
    groups = cols // EDGE
    each = planes // groups
    packed = pack_edge([out_ref[each * g : each * (g + 1)].reshape(each * rows, cols) for g in range(groups)])
    edge_ref[...] = packed.reshape(edge_ref.shape)


def far_kernel(low_ref, high_ref, est_ref, mat_ya, mat_xa, mat_x, mat_y, est_out, corr_out, part_out):
    planes, rows, cols = est_ref.shape
    groups = cols // EDGE
    each = planes // groups
    size = each * rows
    corr_out[...] = jnp.zeros(corr_out.shape, F32)

    def step(pair, carry):
        both = [(2 * pair + side, pl.ds(each * (2 * pair + side), each)) for side in range(2)]
        block = jnp.concatenate([joined_rows(low_ref, high_ref, at) for _, at in both], axis=1)
        block = times_left(mat_ya, block)
        wide = []
        for side, (g, at) in enumerate(both):
            corr = times_right(block[:, cols * side : cols * (side + 1)], mat_xa.at[g])
            corr_out[...] += corr[:, cols:]
            est = est_ref[at].reshape(size, cols) * corr[:, :cols]
            est_out[at] = est.reshape(each, rows, cols)
            if part_out is not None:
                wide.append(times_right(est, mat_x))
        if part_out is not None:
            part = times_left(mat_y, jnp.concatenate(wide, axis=1))
            for side, (_, at) in enumerate(both):
                part_out[at] = part[:, cols * side : cols * (side + 1)].reshape(each, rows, cols)
        return carry

    lax.fori_loop(0, groups // 2, step, 0)


def far_last_kernel(low_ref, high_ref, est_ref, mat_ya, mat_xa, one_out, two_out, corr_out, est):
    far_kernel(low_ref, high_ref, est_ref, mat_ya, mat_xa, None, None, est, corr_out, None)
    half = est.shape[1] // 2
    first = place()[1] == 0
    low, high = est[:, :half], est[:, half:]
    one_out[...] = jnp.where(first, high, low)
    two_out[...] = jnp.where(first, low, high)


def near_window(edge_low, edge_high, corr_ref, window_ref, mat_ya, mat_window):
    edge = times_left(mat_ya, joined_rows(edge_low, edge_high, slice(None)))
    return window_ref[...] * (corr_ref[...] + times_right(edge, mat_window))


def near_kernel(
    edge_low, edge_high, corr_ref, window_ref, part_ref, mat_ya, mat_window, mat_y, mat_around,
    window_out, part_out, core_ref, low_ref, high_ref,
):
    planes, rows, cols = part_ref.shape
    groups = cols // EDGE
    each = planes // groups
    window = near_window(edge_low, edge_high, corr_ref, window_ref, mat_ya, mat_window)
    window_out[...] = window
    blurred = times_left(mat_y, window)
    for pair in range(groups // 2):
        share = times_right(blurred, mat_around.at[pair])
        for side in range(2):
            at = slice(each * (2 * pair + side), each * (2 * pair + side + 1))
            put_rows(
                part_out, at, part_ref[at] + share[:, cols * side : cols * (side + 1)].reshape(each, rows, cols)
            )
    put_sent(part_out, (core_ref.at[0], core_ref.at[1]), low_ref, high_ref)


def near_last_kernel(edge_low, edge_high, corr_ref, window_ref, mat_ya, mat_window, out_ref):
    window = near_window(edge_low, edge_high, corr_ref, window_ref, mat_ya, mat_window)
    each, half, cols = out_ref.shape
    window = window.reshape(each, 2 * half, cols)
    out_ref[...] = jnp.where(place()[1] == 0, window[:, :half], window[:, half:])


def leave_kernel(one_ref, two_ref, kept_ref, window_ref, window_kept_ref, out_ref):
    planes, rows, wide = one_ref.shape
    groups = wide // EDGE
    each = planes // groups
    lower = place()[0] == 0
    one, two = one_ref[...], jnp.where(stays(), kept_ref[...], two_ref[...])
    window = jnp.where(stays(), window_kept_ref[...], window_ref[...]).reshape(each * rows, wide)
    window = jnp.concatenate([window, window], axis=1)
    from_cut = lanes(window.shape, 1) - wide + EDGE // 2
    for g in range(groups):
        at = slice(each * g, each * (g + 1))
        block = jnp.concatenate([jnp.where(lower, two[at], one[at]), jnp.where(lower, one[at], two[at])], axis=2)
        turned = pltpu.roll(window, (wide - EDGE // 2 - EDGE * g) % (2 * wide), 1)
        block = jnp.where((from_cut >= 0) & (from_cut < EDGE), turned, block.reshape(each * rows, 2 * wide))
        out_ref[at] = block.reshape(each, rows, 2 * wide)


def local(estimate_start, view_images, psf_taps):
    planes, rows_dev, cols = estimate_start.shape
    views, _, taps = psf_taps.shape
    half = taps // 2
    n = lax.axis_size("gz") // 2
    rows, wide = rows_dev * lax.axis_size("gy"), cols // 2
    core = lax.axis_index("gy")
    send = lambda value, pairs: lax.ppermute(value, AXES, pairs)
    groups = wide // EDGE
    rows_y = planes * rows // groups
    field, packed, piece = (planes, rows, wide), (rows_y, wide), (planes, rows_dev, wide)
    sent, by_half = (half, rows_dev, wide), (2, *piece)
    sent_both, edge = (2, *sent), (planes // groups, rows_dev, wide)

    pair = lambda *shape: jax.ShapeDtypeStruct(shape, BF16)
    mats_out = [
        pair(groups, 2, wide, 2 * wide),
        pair(2, wide, wide),
        pair(2, wide, wide),
        pair(groups // 2, 2, wide, 2 * wide),
        pair(2, rows_y, rows_y),
        pair(2, rows_y, rows_y),
        (taps, 8, wide),
    ]
    mats_scratch = [pltpu.VMEM((cols, cols), F32)] * 2 + [pltpu.VMEM((1, cols), F32)]

    def pieces(value, *index):
        def cut(half):
            start = (*index, 0, 0, wide * half)
            return lax.dynamic_slice(value, start, (1,) * len(index) + piece).reshape(piece)

        return cut(1 - core), cut(core)

    entry = (planes + planes // groups, rows_dev, wide)
    one, kept = call(cut_kernel, [entry, entry], estimate_start)
    one, two = send(one, entry_one(n)), send(kept, entry_two(n, True))
    back_x, back_window, mat_x, around, mat_y, mat_ya, k_z = call(
        functools.partial(mats_kernel, view=0, rows=rows), mats_out, psf_taps, scratch=mats_scratch
    )
    image = pieces(view_images, 0)
    image = send(image[0], entry_one(n)), send(image[1], entry_two(n, False)), image[1]
    main, window, part, core_low, core_high, *sent_planes = call(
        first_kernel, [field, packed, by_half, sent, sent, sent, sent], one, two, kept, mat_x, around, mat_y
    )

    for view in range(views):
        for step in range(ITERS):
            last = step + 1 == ITERS
            ahead = view + 1 < views
            if ahead and not last:
                images, _ = lax.optimization_barrier((view_images, part))
                next_pieces = pieces(images, view + 1)
            chip = [send(s, chip_swap(n)) for s in sent_planes]
            name = dict(view=view + 1, rows=rows)
            if view == 0 and step == 0:
                own, *next_mats = call(
                    functools.partial(own_z_first_mats_kernel, **name), [by_half, *mats_out], k_z, part,
                    send(core_low, core_swap(n)), send(core_high, core_swap(n)), psf_taps,
                    scratch=mats_scratch + [pltpu.VMEM(sent_both, F32)],
                )
            elif ahead and not last:
                own, *next_mats = call(
                    functools.partial(own_z_mats_kernel, **name), [by_half, *mats_out], k_z, part,
                    send(sent_core, core_swap(n)), psf_taps, scratch=mats_scratch,
                )
            else:
                (own,) = call(
                    functools.partial(own_z_kernel, flip=False), [by_half], k_z, part, send(sent_core, core_swap(n))
                )
            ratio, sent_core, sent_low = call(
                functools.partial(ratio_kernel, side=0), [piece, sent, sent], k_z, own, chip[0], *image
            )
            core_low, chip_low = send(sent_core, core_swap(n)), send(sent_low, chip_swap(n))
            chip_high, _ = lax.optimization_barrier((chip[1], ratio))
            (low,) = call(own_z_half_kernel, [piece], k_z, ratio, core_low)
            ratio, sent_core, sent_high = call(
                functools.partial(ratio_kernel, side=1), [piece, sent, sent], k_z, own, chip_high, *image
            )
            core_high, chip_high = send(sent_core, core_swap(n)), send(sent_high, chip_swap(n))
            low, edge_low = call(back_edge_kernel, [piece, edge], k_z, low, chip_low, cost=10)
            edge_low = send(edge_low, half_swap(n))
            core_high, _ = lax.optimization_barrier((core_high, low))
            (high,) = call(own_z_half_kernel, [piece], k_z, ratio, core_high)
            if ahead:
                if last:
                    next_kept, _ = lax.optimization_barrier((next_kept, low))
                    next_two = send(next_kept, entry_two(n, True))
                else:
                    next_one, next_kept, _ = lax.optimization_barrier((*next_pieces, low))
                    next_one = send(next_one, entry_one(n))
            high, edge_high = call(back_edge_kernel, [piece, edge], k_z, high, chip_high)
            edge_high = send(edge_high, half_swap(n))
            if not ahead:
                high, edge_low = lax.optimization_barrier((high, edge_low))
            if last and view + 1 == views:
                one, kept, corr = call(
                    far_last_kernel, [piece, piece, packed], low, high, main, mat_ya, back_x,
                    scratch=[pltpu.VMEM(field, F32)],
                )
                (window,) = call(
                    near_last_kernel, [edge], edge_low, edge_high, corr, window, mat_ya, back_window, cost=10
                )
                break
            old_back_x, old_back_window, old_ya = back_x, back_window, mat_ya
            if last:
                back_x, back_window, mat_x, around, mat_y, mat_ya, k_z = next_mats
            main, corr, part = call(
                far_kernel, [field, packed, field], low, high, main, old_ya, old_back_x, mat_x, mat_y, cost=1
            )
            if ahead and last:
                corr, next_two = lax.optimization_barrier((corr, next_two))
                image = next_one, next_two, next_kept
            elif ahead:
                corr, next_one = lax.optimization_barrier((corr, next_one))
            window, part, sent_core, *sent_planes = call(
                near_kernel, [packed, by_half, sent_both, sent, sent],
                edge_low, edge_high, corr, window, part, old_ya, old_back_window, mat_y, around,
            )
    (out,) = call(
        leave_kernel, [estimate_start.shape],
        send(one, back(entry_one(n))), send(kept, entry_two(n, True)), kept, send(window, entry_two(n, True)), window,
    )
    return out


def solution(mesh):
    return jax.shard_map(
        local,
        mesh=mesh,
        in_specs=(P(("grp", "gz"), "gy", None), P(None, ("grp", "gz"), "gy", None), P()),
        out_specs=P(("grp", "gz"), "gy", None),
        check_vma=False,
    )
```

```python
import functools

import jax
import jax.numpy as jnp
from jax import lax
from jax.experimental import pallas as pl
from jax.experimental.pallas import tpu as pltpu
from jax.sharding import PartitionSpec as P

ITERS = 2
AXES = ("gz", "gy")
EDGE = 32
F32, BF16 = jnp.float32, jnp.bfloat16


def spot(zp, xp, c):
    return (2 * zp + xp) * 2 + c


def core_swap(n):
    return [(spot(z, x, c), spot(z, x, 1 - c)) for z in range(n) for x in range(2) for c in range(2)]


def half_swap(n):
    return [(spot(z, x, c), spot(z, 1 - x, c)) for z in range(n) for x in range(2) for c in range(2)]


def chip_swap(n):
    pairs = []
    for x in range(2):
        for z in range(n - 1):
            pairs += [(spot(z, x, 1), spot(z + 1, x, 0)), (spot(z + 1, x, 0), spot(z, x, 1))]
        pairs += [(spot(0, x, 0), spot(0, 1 - x, 0)), (spot(n - 1, x, 1), spot(n - 1, 1 - x, 1))]
    return pairs


def entry_one(n):
    pairs = []
    for z in range(n):
        pairs += [
            (spot(z, 0, 1), spot(z, 0, 0)),
            (spot(z, 0, 0), spot(z, 1, 0)),
            (spot(z, 1, 0), spot(z, 1, 1)),
            (spot(z, 1, 1), spot(z, 0, 1)),
        ]
    return pairs


def entry_two(n, over_z):
    pairs = []
    for z in range(n):
        pairs += [(spot(z, 0, 1), spot(z, 1, 0)), (spot(z, 1, 0), spot(z, 0, 1))]
        if over_z and n % 2 == 0:
            pairs += [(spot(z, 0, 0), spot(z ^ 1, 0, 0)), (spot(z, 1, 1), spot(z ^ 1, 1, 1))]
        else:
            pairs += [(spot(z, 0, 0), spot(z, 1, 1)), (spot(z, 1, 1), spot(z, 0, 0))]
    return pairs


def back(pairs):
    return [(target, source) for source, target in pairs]


def toeplitz(row, half):
    size = row.shape[1]
    base = pltpu.roll(jnp.broadcast_to(row, (size, size)), size - half, 1)
    return pltpu.roll(base, 0, 1, stride=1, stride_axis=0)


def taps_row(taps_ref, view, axis, row_ref):
    taps = taps_ref.shape[2]
    row_ref[...] = jnp.zeros(row_ref.shape, F32)
    row_ref[:, :taps] = taps_ref[view, axis : axis + 1, :]
    row = row_ref[...]
    return row / jnp.sum(row, axis=1, keepdims=True)


def put_halves(ref, matrix):
    ref[0], ref[1] = split(matrix)


def lanes(shape, axis):
    return lax.broadcasted_iota(jnp.int32, shape, axis)


def split(value):
    high = value.astype(BF16)
    return high, (value - high.astype(F32)).astype(BF16)


def dot(a, b):
    return jnp.dot(a, b, preferred_element_type=F32)


def times_right(value, mat_ref):
    high, low = split(value)
    if value.shape[1] >= 256:
        return dot(high, mat_ref[0]) + (dot(low, mat_ref[0]) + dot(high, mat_ref[1]))
    twice = jnp.concatenate([mat_ref[0], mat_ref[0]], axis=0)
    return dot(jnp.concatenate([high, low], axis=1), twice) + dot(high, mat_ref[1])


def times_left(mat_ref, value):
    high, low = split(value)
    cols = value.shape[1]
    if cols >= 256:
        return dot(mat_ref[0], high) + (dot(mat_ref[0], low) + dot(mat_ref[1], high))
    both = dot(mat_ref[0], jnp.concatenate([high, low], axis=1))
    return both[:, :cols] + (both[:, cols:] + dot(mat_ref[1], high))


def call(kernel, outs, *args, scratch=(), cost=0):
    def spec(a):
        small = a.ndim == 1
        return pl.BlockSpec(memory_space=pltpu.SMEM if small else pltpu.VMEM)

    return pl.pallas_call(
        kernel,
        out_shape=[jax.ShapeDtypeStruct(s, F32) if isinstance(s, tuple) else s for s in outs],
        in_specs=[spec(a) for a in args],
        out_specs=[pl.BlockSpec(memory_space=pltpu.VMEM) for _ in outs],
        scratch_shapes=list(scratch),
        compiler_params=pltpu.CompilerParams(vmem_limit_bytes=24 * 1024 * 1024),
        cost_estimate=pl.CostEstimate(flops=1 + cost * 10**9, bytes_accessed=1 + cost * 3 * 10**6, transcendentals=0),
    )(*args)


def place():
    core, gz, n = lax.axis_index("gy"), lax.axis_index("gz"), lax.axis_size("gz") // 2
    at_end = ((gz < 2) & (core == 0)) | ((gz >= 2 * n - 2) & (core == 1))
    return core, gz % 2, jnp.where(at_end, 0, 1)


def cut_kernel(est_ref, one_ref, two_ref):
    planes, rows, cols = est_ref.shape
    wide = cols // 2
    groups = wide // EDGE
    each = planes // groups
    lower = place()[0] == 0
    packed = None
    for g in range(groups):
        at = slice(each * g, each * (g + 1))
        block = est_ref[at].reshape(each * rows, cols)
        low, high = block[:, :wide].reshape(each, rows, wide), block[:, wide:].reshape(each, rows, wide)
        one_ref[at] = jnp.where(lower, high, low)
        two_ref[at] = jnp.where(lower, low, high)
        turned = pltpu.roll(block, (EDGE * g - wide + EDGE // 2) % cols, 1)[:, :wide]
        packed = turned if packed is None else jnp.where(lanes(turned.shape, 1) // EDGE == g, turned, packed)
    packed = packed.reshape(each, rows, wide)
    one_ref[planes:] = packed
    two_ref[planes:] = packed


def first_kernel(
    one_ref, two_ref, kept_ref, mat_x, mat_around, mat_y,
    main_out, window_out, part_out, core_low_ref, core_high_ref, low_ref, high_ref,
):
    planes, rows, cols = main_out.shape
    half = rows // 2
    first = place()[1] == 0

    one, two = one_ref[...], jnp.where(stays(), kept_ref[...], two_ref[...])
    low, high = jnp.where(first, two, one), jnp.where(first, one, two)
    main_out[:, :half], main_out[:, half:] = low[:planes], high[:planes]
    groups = cols // EDGE
    each = planes // groups
    size = each * rows
    window = jnp.concatenate([low[planes:], high[planes:]], axis=1).reshape(size, cols)
    window_out[...] = window
    for pair in range(groups // 2):
        both = (2 * pair, 2 * pair + 1)
        blocks = [main_out[each * g : each * (g + 1)].reshape(size, cols) for g in both]
        part = jnp.concatenate([times_right(block, mat_x) for block in blocks], axis=1)
        part = times_left(mat_y, part + times_right(window, mat_around.at[pair]))
        for side, g in enumerate(both):
            put_rows(
                part_out, slice(each * g, each * (g + 1)),
                part[:, cols * side : cols * (side + 1)].reshape(each, rows, cols),
            )
    put_sent(part_out, (core_low_ref, core_high_ref), low_ref, high_ref)


def stays():
    core, xp, _ = place()
    return core == xp


def put_rows(out_ref, at, block):
    rows = out_ref.shape[2]
    out_ref[0, at], out_ref[1, at] = block[:, :rows], block[:, rows:]


def put_sent(out_ref, core_ref, low_ref, high_ref):
    flags = place()
    sent = low_ref.shape[0]
    spare = out_ref.shape[1] - sent
    at = pl.ds((1 - flags[0]) * spare, sent)
    core_ref[0][...], core_ref[1][...] = out_ref[0, at], out_ref[1, at]
    at = pl.ds(flags[0] * spare, sent)
    low_ref[...], high_ref[...] = out_ref[0, at], out_ref[1, at]


def pack_edge(blocks):
    first = jnp.where(place()[1] == 0, EDGE, 0)
    packed = None
    for g, block in enumerate(blocks):
        cols = block.shape[1]
        turned = pltpu.roll(block, (EDGE * g + first) % cols, 1)
        if packed is None:
            packed = turned
        else:
            lane = lax.broadcasted_iota(jnp.int32, block.shape, 1)
            packed = jnp.where(lane // EDGE == g, turned, packed)
    return packed


def mats_kernel(
    taps_ref, back_x_ref, back_window_ref, x_ref, window_ref, y_ref, ya_ref, z_ref,
    full, turned, row_ref, *, view, rows
):
    size, wide = full.shape[0], x_ref.shape[1]
    taps = z_ref.shape[0]
    groups = wide // EDGE
    near = EDGE // 2
    flags = place()
    first = flags[1] == 0
    diff = lanes((size, size), 0) - lanes((size, size), 1)
    band_x = jnp.where(jnp.abs(diff) <= taps // 2, toeplitz(taps_row(taps_ref, view, 2, row_ref), taps // 2), 0.0)
    full[...] = band_x
    turned[...] = band_x.T
    main = pl.ds(pl.multiple_of(flags[1] * wide, wide), wide)
    here = full[main, :]
    block = jnp.where(first, here[:, :wide], here[:, wide:])
    lane = lanes((wide, wide), 1)
    for g in range(groups):
        moved = pltpu.roll(here, (EDGE * g - wide + near) % size, 1)[:, :wide]
        moved = jnp.where(lane // EDGE == g, moved, 0.0)
        put_halves(back_x_ref.at[g], jnp.concatenate([block, moved], axis=1))
    beyond = full[pl.ds(pl.multiple_of(jnp.where(first, wide, wide - EDGE), EDGE), EDGE), :]
    parts = []
    for g in range(groups):
        moved = pltpu.roll(beyond, (EDGE * g - wide + near) % size, 1)[:, :wide]
        parts.append(jnp.where(lanes((EDGE, wide), 1) // EDGE == g, moved, 0.0))
    put_halves(back_window_ref, jnp.concatenate(parts, axis=0))
    here = turned[main, :]
    block = jnp.where(first, here[:, :wide], here[:, wide:])
    row = lanes((wide, wide), 0)
    apart = jnp.where(first, row, row - near)
    put_halves(x_ref, jnp.where((apart >= 0) & (apart < wide - near), block, 0.0))
    around = turned[wide - near : wide + near, :]
    around = jnp.where(first, around[:, :wide], around[:, wide:])
    zero = jnp.zeros((EDGE, wide), F32)
    for pair in range(groups // 2):
        both = [
            jnp.concatenate([around if g == 2 * pair + side else zero for g in range(groups)], axis=0)
            for side in range(2)
        ]
        put_halves(window_ref.at[pair], jnp.concatenate(both, axis=1))
    band_y = toeplitz(taps_row(taps_ref, view, 1, row_ref), taps // 2)
    band_y = jnp.where(lanes((size, size), 0) // rows == lanes((size, size), 1) // rows, band_y, 0.0)
    put_halves(y_ref, band_y)
    put_halves(ya_ref, band_y.T)
    line = taps_row(taps_ref, view, 0, row_ref)
    for tap in range(taps):
        z_ref[tap] = jnp.broadcast_to(line[:, tap : tap + 1], z_ref.shape[1:])


def add_planes(total, taps_ref, field, flip):
    taps = taps_ref.shape[0]
    half = taps // 2
    for tap in range(taps):
        weight = None
        for i in range(len(total)):
            plane = field.get(i + tap - half)
            if plane is None:
                continue
            if weight is None:
                weight = taps_ref[taps - 1 - tap if flip else tap]
            term = weight * plane
            total[i] = term if total[i] is None else total[i] + term
    return total


def own_z_kernel(taps, own_ref, core_ref, out_ref, *, flip):
    parts, planes, rows, _ = own_ref.shape
    flags = place()
    half = taps.shape[0] // 2
    tiles = rows // 8
    for core in range(2):

        @pl.when(flags[0] == core)
        def _():
            def step(i, carry):
                part, at = i // tiles, pl.ds(pl.multiple_of(i % tiles * 8, 8), 8)
                field = {j: own_ref[part, j, at, :] for j in range(planes)}
                for j in range(half):
                    field[planes + j if core == 0 else j - half] = core_ref[part, j, at, :]
                total = add_planes([None] * planes, taps, field, flip)
                for j in range(planes):
                    out_ref[part, j, at, :] = total[j]
                return carry

            lax.fori_loop(0, parts * tiles, step, 0)


def own_z_mats_kernel(taps, own_ref, core_ref, psf_ref, out_ref, *refs, view, rows):
    own_z_kernel(taps, own_ref, core_ref, out_ref, flip=False)
    mats_kernel(psf_ref, *refs, view=view, rows=rows)


def own_z_first_mats_kernel(taps, own_ref, core_low_ref, core_high_ref, psf_ref, out_ref, *refs, view, rows):
    *refs, core_ref = refs
    own_z_first_kernel(taps, own_ref, core_low_ref, core_high_ref, out_ref, core_ref)
    mats_kernel(psf_ref, *refs, view=view, rows=rows)


def own_z_half_kernel(taps, own_ref, core_ref, out_ref):
    grown = (1, *own_ref.shape)
    own_z_kernel(taps, own_ref.reshape(grown), core_ref.reshape(1, *core_ref.shape), out_ref.reshape(grown), flip=True)


def own_z_first_kernel(taps, own_ref, core_low_ref, core_high_ref, out_ref, core_ref):
    core_ref[0], core_ref[1] = core_low_ref[...], core_high_ref[...]
    own_z_kernel(taps, own_ref, core_ref, out_ref, flip=False)


def finish_z(taps, part_ref, chip_ref, flip, put):
    planes, rows, _ = part_ref.shape
    half = chip_ref.shape[0]
    flags = place()
    for case in range(3):
        wanted = (flags[2] == 0) if case == 2 else (flags[2] == 1) & (flags[0] == case)

        @pl.when(wanted)
        def _():
            def step(i, carry):
                at = pl.ds(pl.multiple_of(i * 8, 8), 8)
                total = [part_ref[j, at, :] for j in range(planes)]
                if case < 2:
                    first = -half if case == 0 else planes
                    field = {first + j: chip_ref[j, at, :] for j in range(half)}
                    total = add_planes(total, taps, field, flip)
                put(at, total)
                return carry

            lax.fori_loop(0, rows // 8, step, 0)


def ratio_kernel(taps, part_ref, chip_ref, one_ref, two_ref, kept_ref, out_ref, core_ref, send_ref, *, side):
    planes = part_ref.shape[1]
    flags = place()
    from_two, keep = flags[1] == side, stays()

    def put(at, blurred):
        for j in range(planes):
            two = jnp.where(keep, kept_ref[j, at, :], two_ref[j, at, :])
            out_ref[j, at, :] = jnp.where(from_two, two, one_ref[j, at, :]) / blurred[j]

    finish_z(taps, part_ref.at[side], chip_ref, False, put)
    sent = send_ref.shape[0]
    core_ref[...] = out_ref[pl.ds((1 - flags[0]) * (planes - sent), sent)]
    send_ref[...] = out_ref[pl.ds(flags[0] * (planes - sent), sent)]


def back_kernel(taps, part_ref, chip_ref, out_ref):
    def put(at, total):
        for j in range(len(total)):
            out_ref[j, at, :] = total[j]

    finish_z(taps, part_ref, chip_ref, True, put)


def joined_rows(low_ref, high_ref, at):
    block = jnp.concatenate([low_ref[at], high_ref[at]], axis=1)
    return block.reshape(block.shape[0] * block.shape[1], block.shape[2])


def back_edge_kernel(taps, part_ref, chip_ref, out_ref, edge_ref):
    back_kernel(taps, part_ref, chip_ref, out_ref)
    planes, rows, cols = out_ref.shape
    groups = cols // EDGE
    each = planes // groups
    packed = pack_edge([out_ref[each * g : each * (g + 1)].reshape(each * rows, cols) for g in range(groups)])
    edge_ref[...] = packed.reshape(edge_ref.shape)


def far_kernel(low_ref, high_ref, est_ref, mat_ya, mat_xa, mat_x, mat_y, est_out, corr_out, part_out):
    planes, rows, cols = est_ref.shape
    groups = cols // EDGE
    each = planes // groups
    size = each * rows
    corr_out[...] = jnp.zeros(corr_out.shape, F32)

    def step(pair, carry):
        both = [(2 * pair + side, pl.ds(each * (2 * pair + side), each)) for side in range(2)]
        block = jnp.concatenate([joined_rows(low_ref, high_ref, at) for _, at in both], axis=1)
        block = times_left(mat_ya, block)
        wide = []
        for side, (g, at) in enumerate(both):
            corr = times_right(block[:, cols * side : cols * (side + 1)], mat_xa.at[g])
            corr_out[...] += corr[:, cols:]
            est = est_ref[at].reshape(size, cols) * corr[:, :cols]
            est_out[at] = est.reshape(each, rows, cols)
            if part_out is not None:
                wide.append(times_right(est, mat_x))
        if part_out is not None:
            part = times_left(mat_y, jnp.concatenate(wide, axis=1))
            for side, (_, at) in enumerate(both):
                part_out[at] = part[:, cols * side : cols * (side + 1)].reshape(each, rows, cols)
        return carry

    lax.fori_loop(0, groups // 2, step, 0)


def far_last_kernel(low_ref, high_ref, est_ref, window_ref, mat_ya, mat_xa, one_out, two_out, est, corr):
    far_kernel(low_ref, high_ref, est_ref, mat_ya, mat_xa, None, None, est, corr, None)
    planes, rows, cols = est.shape
    half = rows // 2
    first = place()[1] == 0
    window = (window_ref[...] * corr[...]).reshape(-1, rows, cols)
    for block, at in ((est[...], slice(0, planes)), (window, slice(planes, None))):
        low, high = block[:, :half], block[:, half:]
        one_out[at] = jnp.where(first, high, low)
        two_out[at] = jnp.where(first, low, high)


def near_window(edge_low, edge_high, corr_ref, window_ref, mat_ya, mat_window):
    edge = times_left(mat_ya, joined_rows(edge_low, edge_high, slice(None)))
    return window_ref[...] * (corr_ref[...] + times_right(edge, mat_window))


def near_kernel(
    edge_low, edge_high, corr_ref, window_ref, part_ref, mat_ya, mat_window, mat_y, mat_around,
    window_out, part_out, core_ref, low_ref, high_ref,
):
    planes, rows, cols = part_ref.shape
    groups = cols // EDGE
    each = planes // groups
    window = near_window(edge_low, edge_high, corr_ref, window_ref, mat_ya, mat_window)
    window_out[...] = window
    blurred = times_left(mat_y, window)
    for pair in range(groups // 2):
        share = times_right(blurred, mat_around.at[pair])
        for side in range(2):
            at = slice(each * (2 * pair + side), each * (2 * pair + side + 1))
            put_rows(
                part_out, at, part_ref[at] + share[:, cols * side : cols * (side + 1)].reshape(each, rows, cols)
            )
    put_sent(part_out, (core_ref.at[0], core_ref.at[1]), low_ref, high_ref)


def leave_kernel(one_ref, two_ref, kept_ref, out_ref):
    planes, rows, cols = out_ref.shape
    wide = cols // 2
    groups = wide // EDGE
    each = planes // groups
    lower = place()[0] == 0
    one, two = one_ref[...], jnp.where(stays(), kept_ref[...], two_ref[...])
    window = (one[planes:] + two[planes:]).reshape(each * rows, wide)
    window = jnp.concatenate([window, window], axis=1)
    from_cut = lanes(window.shape, 1) - wide + EDGE // 2
    for g in range(groups):
        at = slice(each * g, each * (g + 1))
        block = jnp.concatenate([jnp.where(lower, two[at], one[at]), jnp.where(lower, one[at], two[at])], axis=2)
        turned = pltpu.roll(window, (wide - EDGE // 2 - EDGE * g) % cols, 1)
        block = jnp.where((from_cut >= 0) & (from_cut < EDGE), turned, block.reshape(each * rows, cols))
        out_ref[at] = block.reshape(each, rows, cols)


def local(estimate_start, view_images, psf_taps):
    planes, rows_dev, cols = estimate_start.shape
    views, _, taps = psf_taps.shape
    half = taps // 2
    n = lax.axis_size("gz") // 2
    rows, wide = rows_dev * lax.axis_size("gy"), cols // 2
    core = lax.axis_index("gy")
    send = lambda value, pairs: lax.ppermute(value, AXES, pairs)
    groups = wide // EDGE
    rows_y = planes * rows // groups
    field, packed, piece = (planes, rows, wide), (rows_y, wide), (planes, rows_dev, wide)
    sent, by_half = (half, rows_dev, wide), (2, *piece)
    sent_both, edge = (2, *sent), (planes // groups, rows_dev, wide)

    pair = lambda *shape: jax.ShapeDtypeStruct(shape, BF16)
    mats_out = [
        pair(groups, 2, wide, 2 * wide),
        pair(2, wide, wide),
        pair(2, wide, wide),
        pair(groups // 2, 2, wide, 2 * wide),
        pair(2, rows_y, rows_y),
        pair(2, rows_y, rows_y),
        (taps, 8, wide),
    ]
    mats_scratch = [pltpu.VMEM((cols, cols), F32)] * 2 + [pltpu.VMEM((1, cols), F32)]

    def pieces(value, *index):
        def cut(half):
            start = (*index, 0, 0, wide * half)
            return lax.dynamic_slice(value, start, (1,) * len(index) + piece).reshape(piece)

        return cut(1 - core), cut(core)

    entry = (planes + planes // groups, rows_dev, wide)
    one, kept = call(cut_kernel, [entry, entry], estimate_start)
    one, two = send(one, entry_one(n)), send(kept, entry_two(n, True))
    back_x, back_window, mat_x, around, mat_y, mat_ya, k_z = call(
        functools.partial(mats_kernel, view=0, rows=rows), mats_out, psf_taps, scratch=mats_scratch
    )
    image = pieces(view_images, 0)
    image = send(image[0], entry_one(n)), send(image[1], entry_two(n, False)), image[1]
    main, window, part, core_low, core_high, *sent_planes = call(
        first_kernel, [field, packed, by_half, sent, sent, sent, sent], one, two, kept, mat_x, around, mat_y
    )

    for view in range(views):
        for step in range(ITERS):
            last = step + 1 == ITERS
            ahead = view + 1 < views
            if ahead and not last:
                images, _ = lax.optimization_barrier((view_images, part))
                next_pieces = pieces(images, view + 1)
            chip = [send(s, chip_swap(n)) for s in sent_planes]
            name = dict(view=view + 1, rows=rows)
            if view == 0 and step == 0:
                own, *next_mats = call(
                    functools.partial(own_z_first_mats_kernel, **name), [by_half, *mats_out], k_z, part,
                    send(core_low, core_swap(n)), send(core_high, core_swap(n)), psf_taps,
                    scratch=mats_scratch + [pltpu.VMEM(sent_both, F32)],
                )
            elif ahead and not last:
                own, *next_mats = call(
                    functools.partial(own_z_mats_kernel, **name), [by_half, *mats_out], k_z, part,
                    send(sent_core, core_swap(n)), psf_taps, scratch=mats_scratch,
                )
            else:
                (own,) = call(
                    functools.partial(own_z_kernel, flip=False), [by_half], k_z, part, send(sent_core, core_swap(n))
                )
            ratio, sent_core, sent_low = call(
                functools.partial(ratio_kernel, side=0), [piece, sent, sent], k_z, own, chip[0], *image
            )
            core_low, chip_low = send(sent_core, core_swap(n)), send(sent_low, chip_swap(n))
            chip_high, _ = lax.optimization_barrier((chip[1], ratio))
            (low,) = call(own_z_half_kernel, [piece], k_z, ratio, core_low)
            ratio, sent_core, sent_high = call(
                functools.partial(ratio_kernel, side=1), [piece, sent, sent], k_z, own, chip_high, *image
            )
            core_high, chip_high = send(sent_core, core_swap(n)), send(sent_high, chip_swap(n))
            if last and view + 1 == views:
                (low,) = call(back_kernel, [piece], k_z, low, chip_low, cost=10)
            else:
                low, edge_low = call(back_edge_kernel, [piece, edge], k_z, low, chip_low, cost=10)
                edge_low = send(edge_low, half_swap(n))
            core_high, _ = lax.optimization_barrier((core_high, low))
            (high,) = call(own_z_half_kernel, [piece], k_z, ratio, core_high)
            if ahead:
                if last:
                    next_kept, _ = lax.optimization_barrier((next_kept, low))
                    next_two = send(next_kept, entry_two(n, True))
                else:
                    next_one, next_kept, _ = lax.optimization_barrier((*next_pieces, low))
                    next_one = send(next_one, entry_one(n))
            if last and view + 1 == views:
                (high,) = call(back_kernel, [piece], k_z, high, chip_high)
                one, kept = call(
                    far_last_kernel, [entry, entry], low, high, main, window, mat_ya, back_x,
                    scratch=[pltpu.VMEM(field, F32), pltpu.VMEM(packed, F32)],
                )
                break
            high, edge_high = call(back_edge_kernel, [piece, edge], k_z, high, chip_high)
            edge_high = send(edge_high, half_swap(n))
            if not ahead:
                high, edge_low = lax.optimization_barrier((high, edge_low))
            old_back_x, old_back_window, old_ya = back_x, back_window, mat_ya
            if last:
                back_x, back_window, mat_x, around, mat_y, mat_ya, k_z = next_mats
            main, corr, part = call(
                far_kernel, [field, packed, field], low, high, main, old_ya, old_back_x, mat_x, mat_y, cost=1
            )
            if ahead and last:
                corr, next_two = lax.optimization_barrier((corr, next_two))
                image = next_one, next_two, next_kept
            elif ahead:
                corr, next_one = lax.optimization_barrier((corr, next_one))
            window, part, sent_core, *sent_planes = call(
                near_kernel, [packed, by_half, sent_both, sent, sent],
                edge_low, edge_high, corr, window, part, old_ya, old_back_window, mat_y, around,
            )
    (out,) = call(
        leave_kernel, [estimate_start.shape], send(one, back(entry_one(n))), send(kept, entry_two(n, True)), kept
    )
    return out


def solution(mesh):
    return jax.shard_map(
        local,
        mesh=mesh,
        in_specs=(P(("grp", "gz"), "gy", None), P(None, ("grp", "gz"), "gy", None), P()),
        out_specs=P(("grp", "gz"), "gy", None),
        check_vma=False,
    )
```

```python
import functools

import jax
import jax.numpy as jnp
from jax import lax
from jax.experimental import pallas as pl
from jax.experimental.pallas import tpu as pltpu
from jax.sharding import PartitionSpec as P

ITERS = 2
AXES = ("gz", "gy")
EDGE = 32
F32, BF16 = jnp.float32, jnp.bfloat16


def spot(zp, xp, c):
    return (2 * zp + xp) * 2 + c


def core_swap(n):
    return [(spot(z, x, c), spot(z, x, 1 - c)) for z in range(n) for x in range(2) for c in range(2)]


def half_swap(n):
    return [(spot(z, x, c), spot(z, 1 - x, c)) for z in range(n) for x in range(2) for c in range(2)]


def chip_swap(n):
    pairs = []
    for x in range(2):
        for z in range(n - 1):
            pairs += [(spot(z, x, 1), spot(z + 1, x, 0)), (spot(z + 1, x, 0), spot(z, x, 1))]
        pairs += [(spot(0, x, 0), spot(0, 1 - x, 0)), (spot(n - 1, x, 1), spot(n - 1, 1 - x, 1))]
    return pairs


def entry_one(n):
    pairs = []
    for z in range(n):
        pairs += [
            (spot(z, 0, 1), spot(z, 0, 0)),
            (spot(z, 0, 0), spot(z, 1, 0)),
            (spot(z, 1, 0), spot(z, 1, 1)),
            (spot(z, 1, 1), spot(z, 0, 1)),
        ]
    return pairs


def entry_two(n, over_z):
    pairs = []
    for z in range(n):
        pairs += [(spot(z, 0, 1), spot(z, 1, 0)), (spot(z, 1, 0), spot(z, 0, 1))]
        if over_z and n % 2 == 0:
            pairs += [(spot(z, 0, 0), spot(z ^ 1, 0, 0)), (spot(z, 1, 1), spot(z ^ 1, 1, 1))]
        else:
            pairs += [(spot(z, 0, 0), spot(z, 1, 1)), (spot(z, 1, 1), spot(z, 0, 0))]
    return pairs


def back(pairs):
    return [(target, source) for source, target in pairs]


def toeplitz(row, half):
    size = row.shape[1]
    base = pltpu.roll(jnp.broadcast_to(row, (size, size)), size - half, 1)
    return pltpu.roll(base, 0, 1, stride=1, stride_axis=0)


def taps_row(taps_ref, view, axis, row_ref):
    taps = taps_ref.shape[2]
    row_ref[...] = jnp.zeros(row_ref.shape, F32)
    row_ref[:, :taps] = taps_ref[view, axis : axis + 1, :]
    row = row_ref[...]
    return row / jnp.sum(row, axis=1, keepdims=True)


def put_halves(ref, matrix):
    ref[0], ref[1] = split(matrix)


def lanes(shape, axis):
    return lax.broadcasted_iota(jnp.int32, shape, axis)


def split(value):
    high = value.astype(BF16)
    return high, (value - high.astype(F32)).astype(BF16)


def dot(a, b):
    return jnp.dot(a, b, preferred_element_type=F32)


def times_right(value, mat_ref):
    high, low = split(value)
    if value.shape[1] >= 256:
        return dot(high, mat_ref[0]) + (dot(low, mat_ref[0]) + dot(high, mat_ref[1]))
    twice = jnp.concatenate([mat_ref[0], mat_ref[0]], axis=0)
    return dot(jnp.concatenate([high, low], axis=1), twice) + dot(high, mat_ref[1])


def times_left(mat_ref, value):
    high, low = split(value)
    cols = value.shape[1]
    if cols >= 256:
        return dot(mat_ref[0], high) + (dot(mat_ref[0], low) + dot(mat_ref[1], high))
    both = dot(mat_ref[0], jnp.concatenate([high, low], axis=1))
    return both[:, :cols] + (both[:, cols:] + dot(mat_ref[1], high))


def call(kernel, outs, *args, scratch=(), cost=0):
    def spec(a):
        small = a.ndim == 1
        return pl.BlockSpec(memory_space=pltpu.SMEM if small else pltpu.VMEM)

    return pl.pallas_call(
        kernel,
        out_shape=[jax.ShapeDtypeStruct(s, F32) if isinstance(s, tuple) else s for s in outs],
        in_specs=[spec(a) for a in args],
        out_specs=[pl.BlockSpec(memory_space=pltpu.VMEM) for _ in outs],
        scratch_shapes=list(scratch),
        compiler_params=pltpu.CompilerParams(vmem_limit_bytes=24 * 1024 * 1024),
        cost_estimate=pl.CostEstimate(flops=1 + cost * 10**9, bytes_accessed=1 + cost * 3 * 10**6, transcendentals=0),
    )(*args)


def place():
    core, gz, n = lax.axis_index("gy"), lax.axis_index("gz"), lax.axis_size("gz") // 2
    at_end = ((gz < 2) & (core == 0)) | ((gz >= 2 * n - 2) & (core == 1))
    return core, gz % 2, jnp.where(at_end, 0, 1)


def cut_kernel(est_ref, one_ref, two_ref):
    planes, rows, cols = est_ref.shape
    wide = cols // 2
    groups = wide // EDGE
    each = planes // groups
    lower = place()[0] == 0
    packed = None
    for g in range(groups):
        at = slice(each * g, each * (g + 1))
        block = est_ref[at].reshape(each * rows, cols)
        low, high = block[:, :wide].reshape(each, rows, wide), block[:, wide:].reshape(each, rows, wide)
        one_ref[at] = jnp.where(lower, high, low)
        two_ref[at] = jnp.where(lower, low, high)
        turned = pltpu.roll(block, (EDGE * g - wide + EDGE // 2) % cols, 1)[:, :wide]
        packed = turned if packed is None else jnp.where(lanes(turned.shape, 1) // EDGE == g, turned, packed)
    packed = packed.reshape(each, rows, wide)
    one_ref[planes:] = packed
    two_ref[planes:] = packed


def first_kernel(
    one_ref, two_ref, kept_ref, mat_x, mat_around, mat_y,
    main_out, window_out, part_out, core_low_ref, core_high_ref, low_ref, high_ref,
):
    planes, rows, cols = main_out.shape
    half = rows // 2
    first = place()[1] == 0

    one, two = one_ref[...], jnp.where(stays(), kept_ref[...], two_ref[...])
    low, high = jnp.where(first, two, one), jnp.where(first, one, two)
    main_out[:, :half], main_out[:, half:] = low[:planes], high[:planes]
    groups = cols // EDGE
    each = planes // groups
    size = each * rows
    window = jnp.concatenate([low[planes:], high[planes:]], axis=1).reshape(size, cols)
    window_out[...] = window
    for pair in range(groups // 2):
        both = (2 * pair, 2 * pair + 1)
        blocks = [main_out[each * g : each * (g + 1)].reshape(size, cols) for g in both]
        part = jnp.concatenate([times_right(block, mat_x) for block in blocks], axis=1)
        part = times_left(mat_y, part + times_right(window, mat_around.at[pair]))
        for side, g in enumerate(both):
            put_rows(
                part_out, slice(each * g, each * (g + 1)),
                part[:, cols * side : cols * (side + 1)].reshape(each, rows, cols),
            )
    put_sent(part_out, (core_low_ref, core_high_ref), low_ref, high_ref)


def stays():
    core, xp, _ = place()
    return core == xp


def put_rows(out_ref, at, block):
    rows = out_ref.shape[2]
    out_ref[0, at], out_ref[1, at] = block[:, :rows], block[:, rows:]


def put_sent(out_ref, core_ref, low_ref, high_ref):
    flags = place()
    sent = low_ref.shape[0]
    spare = out_ref.shape[1] - sent
    at = pl.ds((1 - flags[0]) * spare, sent)
    core_ref[0][...], core_ref[1][...] = out_ref[0, at], out_ref[1, at]
    at = pl.ds(flags[0] * spare, sent)
    low_ref[...], high_ref[...] = out_ref[0, at], out_ref[1, at]


def pack_edge(blocks):
    first = jnp.where(place()[1] == 0, EDGE, 0)
    packed = None
    for g, block in enumerate(blocks):
        cols = block.shape[1]
        turned = pltpu.roll(block, (EDGE * g + first) % cols, 1)
        if packed is None:
            packed = turned
        else:
            lane = lax.broadcasted_iota(jnp.int32, block.shape, 1)
            packed = jnp.where(lane // EDGE == g, turned, packed)
    return packed


def mats_kernel(
    taps_ref, back_x_ref, back_window_ref, x_ref, window_ref, y_ref, ya_ref, z_ref,
    full, turned, row_ref, *, view, rows
):
    size, wide = full.shape[0], x_ref.shape[1]
    taps = z_ref.shape[0]
    groups = wide // EDGE
    near = EDGE // 2
    flags = place()
    first = flags[1] == 0
    diff = lanes((size, size), 0) - lanes((size, size), 1)
    band_x = jnp.where(jnp.abs(diff) <= taps // 2, toeplitz(taps_row(taps_ref, view, 2, row_ref), taps // 2), 0.0)
    full[...] = band_x
    turned[...] = band_x.T
    main = pl.ds(pl.multiple_of(flags[1] * wide, wide), wide)
    here = full[main, :]
    block = jnp.where(first, here[:, :wide], here[:, wide:])
    lane = lanes((wide, wide), 1)
    for g in range(groups):
        moved = pltpu.roll(here, (EDGE * g - wide + near) % size, 1)[:, :wide]
        moved = jnp.where(lane // EDGE == g, moved, 0.0)
        put_halves(back_x_ref.at[g], jnp.concatenate([block, moved], axis=1))
    beyond = full[pl.ds(pl.multiple_of(jnp.where(first, wide, wide - EDGE), EDGE), EDGE), :]
    parts = []
    for g in range(groups):
        moved = pltpu.roll(beyond, (EDGE * g - wide + near) % size, 1)[:, :wide]
        parts.append(jnp.where(lanes((EDGE, wide), 1) // EDGE == g, moved, 0.0))
    put_halves(back_window_ref, jnp.concatenate(parts, axis=0))
    here = turned[main, :]
    block = jnp.where(first, here[:, :wide], here[:, wide:])
    row = lanes((wide, wide), 0)
    apart = jnp.where(first, row, row - near)
    put_halves(x_ref, jnp.where((apart >= 0) & (apart < wide - near), block, 0.0))
    around = turned[wide - near : wide + near, :]
    around = jnp.where(first, around[:, :wide], around[:, wide:])
    zero = jnp.zeros((EDGE, wide), F32)
    for pair in range(groups // 2):
        both = [
            jnp.concatenate([around if g == 2 * pair + side else zero for g in range(groups)], axis=0)
            for side in range(2)
        ]
        put_halves(window_ref.at[pair], jnp.concatenate(both, axis=1))
    band_y = toeplitz(taps_row(taps_ref, view, 1, row_ref), taps // 2)
    band_y = jnp.where(lanes((size, size), 0) // rows == lanes((size, size), 1) // rows, band_y, 0.0)
    put_halves(y_ref, band_y)
    put_halves(ya_ref, band_y.T)
    line = taps_row(taps_ref, view, 0, row_ref)
    for tap in range(taps):
        z_ref[tap] = jnp.broadcast_to(line[:, tap : tap + 1], z_ref.shape[1:])


def add_planes(total, taps_ref, field, flip):
    taps = taps_ref.shape[0]
    half = taps // 2
    for tap in range(taps):
        weight = None
        for i in range(len(total)):
            plane = field.get(i + tap - half)
            if plane is None:
                continue
            if weight is None:
                weight = taps_ref[taps - 1 - tap if flip else tap]
            term = weight * plane
            total[i] = term if total[i] is None else total[i] + term
    return total


def own_z_kernel(taps, own_ref, core_ref, out_ref, *, flip):
    parts, planes, rows, _ = own_ref.shape
    flags = place()
    half = taps.shape[0] // 2
    tiles = rows // 8
    for core in range(2):

        @pl.when(flags[0] == core)
        def _():
            def step(i, carry):
                part, at = i // tiles, pl.ds(pl.multiple_of(i % tiles * 8, 8), 8)
                field = {j: own_ref[part, j, at, :] for j in range(planes)}
                for j in range(half):
                    field[planes + j if core == 0 else j - half] = core_ref[part, j, at, :]
                total = add_planes([None] * planes, taps, field, flip)
                for j in range(planes):
                    out_ref[part, j, at, :] = total[j]
                return carry

            lax.fori_loop(0, parts * tiles, step, 0)


def own_z_mats_kernel(taps, own_ref, core_ref, psf_ref, out_ref, *refs, view, rows):
    own_z_kernel(taps, own_ref, core_ref, out_ref, flip=False)
    mats_kernel(psf_ref, *refs, view=view, rows=rows)


def own_z_first_mats_kernel(taps, own_ref, core_low_ref, core_high_ref, psf_ref, out_ref, *refs, view, rows):
    *refs, core_ref = refs
    own_z_first_kernel(taps, own_ref, core_low_ref, core_high_ref, out_ref, core_ref)
    mats_kernel(psf_ref, *refs, view=view, rows=rows)


def own_z_half_kernel(taps, own_ref, core_ref, out_ref):
    grown = (1, *own_ref.shape)
    own_z_kernel(taps, own_ref.reshape(grown), core_ref.reshape(1, *core_ref.shape), out_ref.reshape(grown), flip=True)


def own_z_first_kernel(taps, own_ref, core_low_ref, core_high_ref, out_ref, core_ref):
    core_ref[0], core_ref[1] = core_low_ref[...], core_high_ref[...]
    own_z_kernel(taps, own_ref, core_ref, out_ref, flip=False)


def finish_z(taps, part_ref, chip_ref, flip, put):
    planes, rows, _ = part_ref.shape
    half = chip_ref.shape[0]
    flags = place()
    for case in range(3):
        wanted = (flags[2] == 0) if case == 2 else (flags[2] == 1) & (flags[0] == case)

        @pl.when(wanted)
        def _():
            def step(i, carry):
                at = pl.ds(pl.multiple_of(i * 8, 8), 8)
                total = [part_ref[j, at, :] for j in range(planes)]
                if case < 2:
                    first = -half if case == 0 else planes
                    field = {first + j: chip_ref[j, at, :] for j in range(half)}
                    total = add_planes(total, taps, field, flip)
                put(at, total)
                return carry

            lax.fori_loop(0, rows // 8, step, 0)


def ratio_kernel(taps, part_ref, chip_ref, one_ref, two_ref, kept_ref, out_ref, core_ref, send_ref, *, side):
    planes = part_ref.shape[1]
    flags = place()
    from_two, keep = flags[1] == side, stays()

    def put(at, blurred):
        for j in range(planes):
            two = jnp.where(keep, kept_ref[j, at, :], two_ref[j, at, :])
            out_ref[j, at, :] = jnp.where(from_two, two, one_ref[j, at, :]) / blurred[j]

    finish_z(taps, part_ref.at[side], chip_ref, False, put)
    sent = send_ref.shape[0]
    core_ref[...] = out_ref[pl.ds((1 - flags[0]) * (planes - sent), sent)]
    send_ref[...] = out_ref[pl.ds(flags[0] * (planes - sent), sent)]


def back_kernel(taps, part_ref, chip_ref, out_ref):
    def put(at, total):
        for j in range(len(total)):
            out_ref[j, at, :] = total[j]

    finish_z(taps, part_ref, chip_ref, True, put)


def joined_rows(low_ref, high_ref, at):
    block = jnp.concatenate([low_ref[at], high_ref[at]], axis=1)
    return block.reshape(block.shape[0] * block.shape[1], block.shape[2])


def back_edge_kernel(taps, part_ref, chip_ref, out_ref, edge_ref):
    back_kernel(taps, part_ref, chip_ref, out_ref)
    planes, rows, cols = out_ref.shape
    groups = cols // EDGE
    each = planes // groups
    packed = pack_edge([out_ref[each * g : each * (g + 1)].reshape(each * rows, cols) for g in range(groups)])
    edge_ref[...] = packed.reshape(edge_ref.shape)


def far_kernel(low_ref, high_ref, est_ref, mat_ya, mat_xa, mat_x, mat_y, est_out, corr_out, part_out):
    planes, rows, cols = est_ref.shape
    groups = cols // EDGE
    each = planes // groups
    size = each * rows
    corr_out[...] = jnp.zeros(corr_out.shape, F32)

    def step(pair, carry):
        both = [(2 * pair + side, pl.ds(each * (2 * pair + side), each)) for side in range(2)]
        block = jnp.concatenate([joined_rows(low_ref, high_ref, at) for _, at in both], axis=1)
        block = times_left(mat_ya, block)
        wide = []
        for side, (g, at) in enumerate(both):
            corr = times_right(block[:, cols * side : cols * (side + 1)], mat_xa.at[g])
            corr_out[...] += corr[:, cols:]
            est = est_ref[at].reshape(size, cols) * corr[:, :cols]
            est_out[at] = est.reshape(each, rows, cols)
            if part_out is not None:
                wide.append(times_right(est, mat_x))
        if part_out is not None:
            part = times_left(mat_y, jnp.concatenate(wide, axis=1))
            for side, (_, at) in enumerate(both):
                part_out[at] = part[:, cols * side : cols * (side + 1)].reshape(each, rows, cols)
        return carry

    lax.fori_loop(0, groups // 2, step, 0)


def far_last_kernel(low_ref, high_ref, est_ref, window_ref, mat_ya, mat_xa, one_out, two_out, est, corr):
    far_kernel(low_ref, high_ref, est_ref, mat_ya, mat_xa, None, None, est, corr, None)
    planes, rows, cols = est.shape
    half = rows // 2
    first = place()[1] == 0
    window = (window_ref[...] * corr[...]).reshape(-1, rows, cols)
    for block, at in ((est[...], slice(0, planes)), (window, slice(planes, None))):
        low, high = block[:, :half], block[:, half:]
        one_out[at] = jnp.where(first, high, low)
        two_out[at] = jnp.where(first, low, high)


def near_window(edge_low, edge_high, corr_ref, window_ref, mat_ya, mat_window):
    edge = times_left(mat_ya, joined_rows(edge_low, edge_high, slice(None)))
    return window_ref[...] * (corr_ref[...] + times_right(edge, mat_window))


def near_kernel(
    edge_low, edge_high, corr_ref, window_ref, part_ref, mat_ya, mat_window, mat_y, mat_around,
    window_out, part_out, core_ref, low_ref, high_ref,
):
    planes, rows, cols = part_ref.shape
    groups = cols // EDGE
    each = planes // groups
    window = near_window(edge_low, edge_high, corr_ref, window_ref, mat_ya, mat_window)
    window_out[...] = window
    blurred = times_left(mat_y, window)
    for pair in range(groups // 2):
        share = times_right(blurred, mat_around.at[pair])
        for side in range(2):
            at = slice(each * (2 * pair + side), each * (2 * pair + side + 1))
            put_rows(
                part_out, at, part_ref[at] + share[:, cols * side : cols * (side + 1)].reshape(each, rows, cols)
            )
    put_sent(part_out, (core_ref.at[0], core_ref.at[1]), low_ref, high_ref)


def leave_kernel(one_ref, two_ref, kept_ref, out_ref):
    planes, rows, cols = out_ref.shape
    wide = cols // 2
    groups = wide // EDGE
    each = planes // groups
    lower = place()[0] == 0
    one, two = one_ref[...], jnp.where(stays(), kept_ref[...], two_ref[...])
    window = (one[planes:] + two[planes:]).reshape(each * rows, wide)
    window = jnp.concatenate([window, window], axis=1)
    from_cut = lanes(window.shape, 1) - wide + EDGE // 2
    for g in range(groups):
        at = slice(each * g, each * (g + 1))
        block = jnp.concatenate([jnp.where(lower, two[at], one[at]), jnp.where(lower, one[at], two[at])], axis=2)
        turned = pltpu.roll(window, (wide - EDGE // 2 - EDGE * g) % cols, 1)
        block = jnp.where((from_cut >= 0) & (from_cut < EDGE), turned, block.reshape(each * rows, cols))
        out_ref[at] = block.reshape(each, rows, cols)


def local(estimate_start, view_images, psf_taps):
    planes, rows_dev, cols = estimate_start.shape
    views, _, taps = psf_taps.shape
    half = taps // 2
    n = lax.axis_size("gz") // 2
    rows, wide = rows_dev * lax.axis_size("gy"), cols // 2
    core = lax.axis_index("gy")
    send = lambda value, pairs: lax.ppermute(value, AXES, pairs)
    groups = wide // EDGE
    rows_y = planes * rows // groups
    field, packed, piece = (planes, rows, wide), (rows_y, wide), (planes, rows_dev, wide)
    sent, by_half = (half, rows_dev, wide), (2, *piece)
    sent_both, edge = (2, *sent), (planes // groups, rows_dev, wide)

    pair = lambda *shape: jax.ShapeDtypeStruct(shape, BF16)
    mats_out = [
        pair(groups, 2, wide, 2 * wide),
        pair(2, wide, wide),
        pair(2, wide, wide),
        pair(groups // 2, 2, wide, 2 * wide),
        pair(2, rows_y, rows_y),
        pair(2, rows_y, rows_y),
        (taps, 8, wide),
    ]
    mats_scratch = [pltpu.VMEM((cols, cols), F32)] * 2 + [pltpu.VMEM((1, cols), F32)]

    def pieces(value, *index):
        def cut(half):
            start = (*index, 0, 0, wide * half)
            return lax.dynamic_slice(value, start, (1,) * len(index) + piece).reshape(piece)

        return cut(1 - core), cut(core)

    entry = (planes + planes // groups, rows_dev, wide)
    one, kept = call(cut_kernel, [entry, entry], estimate_start)
    one, two = send(one, entry_one(n)), send(kept, entry_two(n, True))
    back_x, back_window, mat_x, around, mat_y, mat_ya, k_z = call(
        functools.partial(mats_kernel, view=0, rows=rows), mats_out, psf_taps, scratch=mats_scratch
    )
    image = pieces(view_images, 0)
    image = send(image[0], entry_one(n)), send(image[1], entry_two(n, True)), image[1]
    main, window, part, core_low, core_high, *sent_planes = call(
        first_kernel, [field, packed, by_half, sent, sent, sent, sent], one, two, kept, mat_x, around, mat_y
    )

    for view in range(views):
        for step in range(ITERS):
            last = step + 1 == ITERS
            ahead = view + 1 < views
            if ahead and not last:
                images, _ = lax.optimization_barrier((view_images, part))
                next_pieces = pieces(images, view + 1)
            chip = [send(s, chip_swap(n)) for s in sent_planes]
            name = dict(view=view + 1, rows=rows)
            if view == 0 and step == 0:
                own, *next_mats = call(
                    functools.partial(own_z_first_mats_kernel, **name), [by_half, *mats_out], k_z, part,
                    send(core_low, core_swap(n)), send(core_high, core_swap(n)), psf_taps,
                    scratch=mats_scratch + [pltpu.VMEM(sent_both, F32)],
                )
            elif ahead and not last:
                own, *next_mats = call(
                    functools.partial(own_z_mats_kernel, **name), [by_half, *mats_out], k_z, part,
                    send(sent_core, core_swap(n)), psf_taps, scratch=mats_scratch,
                )
            else:
                (own,) = call(
                    functools.partial(own_z_kernel, flip=False), [by_half], k_z, part, send(sent_core, core_swap(n))
                )
            ratio, sent_core, sent_low = call(
                functools.partial(ratio_kernel, side=0), [piece, sent, sent], k_z, own, chip[0], *image
            )
            core_low, chip_low = send(sent_core, core_swap(n)), send(sent_low, chip_swap(n))
            chip_high, _ = lax.optimization_barrier((chip[1], ratio))
            (low,) = call(own_z_half_kernel, [piece], k_z, ratio, core_low)
            ratio, sent_core, sent_high = call(
                functools.partial(ratio_kernel, side=1), [piece, sent, sent], k_z, own, chip_high, *image
            )
            core_high, chip_high = send(sent_core, core_swap(n)), send(sent_high, chip_swap(n))
            if last and view + 1 == views:
                (low,) = call(back_kernel, [piece], k_z, low, chip_low, cost=10)
            else:
                low, edge_low = call(back_edge_kernel, [piece, edge], k_z, low, chip_low, cost=10)
                edge_low = send(edge_low, half_swap(n))
            core_high, _ = lax.optimization_barrier((core_high, low))
            (high,) = call(own_z_half_kernel, [piece], k_z, ratio, core_high)
            if ahead:
                if last:
                    next_kept, _ = lax.optimization_barrier((next_kept, low))
                    next_two = send(next_kept, entry_two(n, True))
                else:
                    next_one, next_kept, _ = lax.optimization_barrier((*next_pieces, low))
                    next_one = send(next_one, entry_one(n))
            if last and view + 1 == views:
                (high,) = call(back_kernel, [piece], k_z, high, chip_high)
                one, kept = call(
                    far_last_kernel, [entry, entry], low, high, main, window, mat_ya, back_x,
                    scratch=[pltpu.VMEM(field, F32), pltpu.VMEM(packed, F32)],
                )
                break
            high, edge_high = call(back_edge_kernel, [piece, edge], k_z, high, chip_high)
            edge_high = send(edge_high, half_swap(n))
            if not ahead:
                high, edge_low = lax.optimization_barrier((high, edge_low))
            old_back_x, old_back_window, old_ya = back_x, back_window, mat_ya
            if last:
                back_x, back_window, mat_x, around, mat_y, mat_ya, k_z = next_mats
            main, corr, part = call(
                far_kernel, [field, packed, field], low, high, main, old_ya, old_back_x, mat_x, mat_y, cost=1
            )
            if ahead and last:
                corr, next_two = lax.optimization_barrier((corr, next_two))
                image = next_one, next_two, next_kept
            elif ahead:
                corr, next_one = lax.optimization_barrier((corr, next_one))
            window, part, sent_core, *sent_planes = call(
                near_kernel, [packed, by_half, sent_both, sent, sent],
                edge_low, edge_high, corr, window, part, old_ya, old_back_window, mat_y, around,
            )
    (out,) = call(
        leave_kernel, [estimate_start.shape], send(one, back(entry_one(n))), send(kept, entry_two(n, True)), kept
    )
    return out


def solution(mesh):
    return jax.shard_map(
        local,
        mesh=mesh,
        in_specs=(P(("grp", "gz"), "gy", None), P(None, ("grp", "gz"), "gy", None), P()),
        out_specs=P(("grp", "gz"), "gy", None),
        check_vma=False,
    )
```
